256 devices in a mesh: row: 16 (over z, core), col: 4 (over x), depth: 4 (over y).
Axes of the slice: x: 4, y: 4, z: 8, core: 2. Of those that a mesh axis runs over, the one named last changes fastest.
Arguments:
- tokens: bfloat16 [1536, 12288], P(('depth', 'col'), 'row'), may hold values from -6 to 6
- weight: bfloat16 [12288, 24576], P('row', 'col'), may hold values from -0.0546875 to 0.0546875
- cotangent: bfloat16 [1536, 24576], P(('depth', 'row'), 'col'), may hold values from -6 to 6
Outputs:
- activated: bfloat16 [1536, 24576], P(('depth', 'row'), 'col')
- grad_tokens: bfloat16 [1536, 12288], P(('depth', 'col'), 'row')
- grad_weight: bfloat16 [12288, 24576], P('row', ('col', 'depth'))
The draws below stay inside these ranges and needn't reach their ends.
All inputs are finite; a program needn't handle non-finite values.
Results may differ from the reference program's by a relative error of at most 0.0049.
Values may be sent and summed in bfloat16 or wider, within the bound.
A program may use at most 128 MiB of HBM per device.

```python
import math
import jax
import jax.numpy as jnp

D = 12288
FF = 24576
TOKENS = 1536


def levels(key, extent, split, smallest, largest):
    gain = 1.0
    for position, blocks in split:
        steps = jax.random.uniform(jax.random.fold_in(jax.random.fold_in(key, 6), position), (blocks,), jnp.float32, smallest / len(split), largest / len(split))
        gain = gain * jnp.repeat(jnp.exp(steps), extent[position] // blocks).reshape((-1,) + (1,) * (len(extent) - 1 - position))
    return gain


def gaussian(own_key, shape, scale, bound, split=(), dtype=jnp.bfloat16):
    values = jax.random.normal(own_key, shape, jnp.float32) * scale
    if len(split) > 0:
        values = levels(own_key, shape, split, -0.22, 0.18) * values
    return jnp.clip(values, min=-bound, max=bound).astype(dtype)


def setup_inputs(seed: int = 0) -> dict:
    splits = jax.random.split(jax.random.key(seed), 4)
    return {
        "tokens": gaussian(splits[0], (TOKENS, D), 1.0, 6.0, ((0, 16), (1, 16))),
        "weight": gaussian(splits[1], (D, FF), D ** -0.5, 0.0546875, ((0, 16), (1, 4))),
        "cotangent": gaussian(splits[2], (TOKENS, FF), 1.0, 6.0, ((0, 64), (1, 4))),
    }


root_coef = math.sqrt(2.0 / math.pi)
cubic_coef = 0.044715

def gelu_tanh(values):
    hyper = jnp.tanh(root_coef * (values + cubic_coef * values * values * values))
    return 0.5 * values * (1.0 + hyper)

def gelu_slope(values):
    hyper = jnp.tanh(root_coef * (values + cubic_coef * values * values * values))
    inner = root_coef * (1.0 + 3.0 * cubic_coef * values * values)
    return 0.5 * (1.0 + hyper) + 0.5 * values * (1.0 - hyper * hyper) * inner

def reference(tokens, weight, cotangent):
    preact = jnp.dot(tokens, weight, preferred_element_type=jnp.float32)
    activated = gelu_tanh(preact).astype(jnp.bfloat16)
    grad_preact = (cotangent.astype(jnp.float32) * gelu_slope(preact)).astype(jnp.bfloat16)
    grad_tokens = jnp.dot(grad_preact, weight.T, preferred_element_type=jnp.float32).astype(jnp.bfloat16)
    grad_weight = jnp.dot(tokens.T, grad_preact, preferred_element_type=jnp.float32).astype(jnp.bfloat16)
    return (activated, grad_tokens, grad_weight)
```

```python
import functools
import math

import jax
import jax.numpy as jnp
from jax import lax
from jax.experimental import pallas as pl
from jax.experimental.pallas import tpu as pltpu
from jax.sharding import PartitionSpec as P

root_coef = math.sqrt(2.0 / math.pi)
cubic_coef = 0.044715

RING = 8
SIDE = 4
SUB = 48
HALF = 768
CHUNK = 2 * HALF
SHARE = 24
PADDED = 32
TILE = 256
f32, bf16 = jnp.float32, jnp.bfloat16


def wrap(value, extent):
    return lax.rem(value + 2 * extent, extent)


def kernel(
    tok, weight, cot, act_out, gt_out, gw_out,
    T, W, W_sib, part, hop, first, cot_send, cot_recv, act_send, act_recv,
    G, TT, GT, y_send, y_recv, x_send, x_recv, x_own,
    local_sem, send_sem, recv_sem,
):
    row, col, dep = (lax.axis_index(name) for name in ("row", "col", "depth"))
    z, k = row // 2, lax.rem(row, 2)
    tau = 1 - 2 * k

    def device(dz=0, dx=0, dy=0, flip=False):
        core = 1 - k if flip else k
        return (2 * wrap(z + dz, RING) + core, wrap(col + dx, SIDE), wrap(dep + dy, SIDE))

    sibling = device(flip=True)
    numbers = {}
    pending = []

    def number(key):
        return numbers.setdefault(key, len(numbers))

    def copy(key, source, target, to):
        n = number(key)
        return pltpu.make_async_remote_copy(
            src_ref=source, dst_ref=target, send_sem=send_sem.at[n], recv_sem=recv_sem.at[n],
            device_id=to, device_id_type=pl.DeviceIdType.MESH,
        )

    def send(key, source, target, to):
        transfer = copy(key, source, target, to)
        transfer.start()
        pending.append(transfer)

    def receive(key, slot):
        copy(key, slot, slot, sibling).wait_recv()

    local = []
    for half in range(2):
        columns = pl.ds(pl.multiple_of(dep * CHUNK + half * HALF, HALF), HALF)
        local.append(pltpu.make_async_copy(weight.at[:, columns], W.at[half], local_sem.at[half]))
    local.append(pltpu.make_async_copy(tok, T.at[0, dep, col], local_sem.at[2]))
    for transfer in local:
        transfer.start()

    partners = [device(dz=1), device(dz=-1), sibling]
    for step in range(1, SIDE):
        partners += [device(dx=step), device(dy=step), device(dy=step, flip=True)]
    barrier = pltpu.get_barrier_semaphore()
    for partner in partners:
        pl.semaphore_signal(barrier, inc=1, device_id=partner, device_id_type=pl.DeviceIdType.MESH)

    gap = jnp.zeros((PADDED - SHARE, HALF), f32)
    for piece in range(SIDE):
        for half in range(2):
            begin = piece * CHUNK + half * HALF
            values = cot[:, begin : begin + HALF].astype(f32)
            cot_send[piece, half] = jnp.concatenate([values, gap], axis=0).astype(bf16)
    pl.semaphore_wait(barrier, len(partners))

    for s in (1, -1):
        send(("xo", s), tok, T.at[0, dep, col], device(dx=s * tau))
        send(("y0", s), tok.at[0], T.at[0, dep, col, 0], device(dy=s * tau))
    send(("k0", 0), tok, T.at[1, dep, col], sibling)
    columns = pl.ds(pl.multiple_of(dep * CHUNK + (1 - k) * HALF, HALF), HALF)
    send("w", weight.at[:, columns], W_sib, sibling)

    def at_col(j):
        return wrap(col + j * tau, SIDE)

    def at_dep(j):
        return wrap(dep + j * tau, SIDE)

    def start_y1(j):
        slot = T.at[0, dep, at_col(j), 1]
        source = tok.at[1] if j == 0 else slot
        for s in (1, -1):
            send(("y1", j, s), source, slot, device(dy=s * tau))

    def relay_y1(j):
        slot = T.at[0, at_dep(-1), at_col(j), 1]
        receive(("y1", j, 1), slot)
        send(("y1r", j), slot, slot, device(dy=tau))

    def start_x0(j):
        slot = T.at[0, at_dep(j), col, 0]
        for s in (1, -1):
            send(("x0", j, s), slot, slot, device(dx=s * tau))

    def relay_x0(j):
        slot = T.at[0, at_dep(j), at_col(-1), 0]
        receive(("x0", j, 1), slot)
        send(("x0r", j), slot, slot, device(dx=tau))

    def to_sibling_block(j):
        slot = T.at[0, dep, at_col(j)]
        send(("k0", j), slot, T.at[1, dep, at_col(j)], sibling)

    start_y1(0)
    slot = T.at[0, dep, at_col(-1)]
    receive(("xo", 1), slot)
    send("xor", slot, slot, device(dx=tau))
    start_y1(-1)
    to_sibling_block(-1)
    slot = T.at[0, at_dep(-1), col, 0]
    receive(("y0", 1), slot)
    send("y0r", slot, slot, device(dy=tau))
    start_x0(-1)
    receive(("xo", -1), T.at[0, dep, at_col(1)])
    start_y1(1)
    to_sibling_block(1)
    receive(("y0", -1), T.at[0, at_dep(1), col, 0])
    start_x0(1)
    relay_y1(0)
    receive("xor", T.at[0, dep, at_col(2)])
    to_sibling_block(2)
    start_y1(2)

    steps = (0, 1, -1, 2)

    def stream(i):
        return wrap(dep + steps[i], SIDE)

    def ring(j):
        return wrap(z + j * tau, RING)

    def partial_preact(i):
        group = stream(i)

        def tile(n, carry):
            lanes = pl.ds(pl.multiple_of(n * TILE, TILE), TILE)
            own = T[0, group].reshape(RING * SUB, HALF)
            other = T[1, group].reshape(RING * SUB, HALF)
            total = jnp.dot(own, W[k, :, lanes], preferred_element_type=f32)
            total += jnp.dot(other, W_sib[:, lanes], preferred_element_type=f32)
            part[i, :, :, lanes] = total.reshape(RING, SUB, TILE)
            return carry

        lax.fori_loop(0, HALF // TILE, tile, 0)

    def enter(i):
        partial_preact(i)
        first[i, 0] = part[i, ring(4)].astype(bf16)
        send(("r", i, 0, 0), first.at[i, 0], hop.at[i, 0, 0], device(dz=tau))
        first[i, 1] = part[i, ring(-3)].astype(bf16)
        send(("r", i, 1, 1), first.at[i, 1], hop.at[i, 1, 1], device(dz=-tau))

    def pass_on(i, way, at, j):
        receive(("r", i, way, at), hop.at[i, way, at])
        hop[i, way, at] = (hop[i, way, at].astype(f32) + part[i, ring(j)]).astype(bf16)
        to = device(dz=tau if way == 0 else -tau)
        send(("r", i, way, at + 1), hop.at[i, way, at], hop.at[i, way, at + 1], to)

    def spread(i, block, ways):
        slot = G.at[block, k, stream(i)]
        for key, to in ways:
            send(key, slot, slot, to)

    def finish(i):
        receive(("r", i, 0, 3), hop.at[i, 0, 3])
        receive(("r", i, 1, 3), hop.at[i, 1, 3])
        v = part[i, z] + hop[i, 0, 3].astype(f32) + hop[i, 1, 3].astype(f32)
        group = stream(i)
        for flip in range(2):
            if i or flip:
                core = 1 - k if flip else k
                receive(("c", -steps[i] % SIDE, flip), cot_recv.at[group, core])
        hyper = jnp.tanh(root_coef * (v + cubic_coef * v * v * v))
        inner = root_coef * (1.0 + 3.0 * cubic_coef * v * v)
        slope = 0.5 * (1.0 + hyper) + 0.5 * v * (1.0 - hyper * hyper) * inner
        given = jnp.concatenate(
            [cot_recv[group, core].astype(f32)[:SHARE] for core in range(2)], axis=0
        )
        G[z, k, group] = (given * slope).astype(bf16)
        spread(i, z, [
            (("g", i, 0, 1), device(dz=tau)), (("g", i, 1, 1), device(dz=-tau)),
            (("s", i, 0), sibling),
        ])
        active = 0.5 * v * (1.0 + hyper)
        for core in range(2):
            mine = active[core * SHARE : (core + 1) * SHARE]
            act_send[group, core] = jnp.concatenate([mine, gap], axis=0).astype(bf16)
        for flip in range(2):
            core = 1 - k if flip else k
            if i == 0 and flip == 0:
                act_recv[dep, k] = act_send[dep, k]
            else:
                send(
                    ("a", steps[i] % SIDE, flip), act_send.at[group, core], act_recv.at[dep, k],
                    device(dy=steps[i], flip=bool(flip)),
                )

    def relay(i, far):
        for way in range(2):
            if way == 1 and far == 4:
                continue
            j = -far if way == 0 else far
            block = ring(j)
            receive(("g", i, way, far), G.at[block, k, stream(i)])
            ways = []
            if far < (4 if way == 0 else 3):
                ways.append((("g", i, way, far + 1), device(dz=tau if way == 0 else -tau)))
            ways.append((("s", i, j), sibling))
            spread(i, block, ways)

    def sibling_blocks():
        for j in (0, -1, 1, 2):
            receive(("k0", j), T.at[1, dep, at_col(-j)])

    for transfer in local:
        transfer.wait()
    receive("w", W_sib)
    sibling_blocks()
    enter(0)

    slot = T.at[0, at_dep(2), col, 0]
    receive("y0r", slot)
    start_x0(2)
    relay_x0(-1)
    relay_x0(1)
    relay_y1(-1)
    relay_y1(1)
    relay_x0(2)
    relay_y1(2)

    for step in range(SIDE):
        for flip in range(2):
            piece = wrap(dep + step, SIDE)
            core = 1 - k if flip else k
            if step == 0 and flip == 0:
                cot_recv[dep, k] = cot_send[dep, k]
            else:
                send(
                    ("c", step, flip), cot_send.at[piece, core], cot_recv.at[dep, k],
                    device(dy=step, flip=bool(flip)),
                )

    pass_on(0, 0, 0, 3)
    pass_on(0, 1, 1, -2)

    for j in (-1, 1):
        receive(("x0", j, -1), T.at[0, at_dep(j), at_col(1), 0])
        receive(("x0r", j), T.at[0, at_dep(j), at_col(2), 0])
    for j in (0, -1, 1, 2):
        receive(("y1", j, -1), T.at[0, at_dep(1), at_col(j), 1])
    for i in (1, 2):
        send(("k", i), T.at[0, stream(i)], T.at[1, stream(i)], sibling)
    receive(("x0", 2, -1), T.at[0, at_dep(2), at_col(1), 0])
    receive(("x0r", 2), T.at[0, at_dep(2), at_col(2), 0])
    for j in (0, -1, 1, 2):
        receive(("y1r", j), T.at[0, at_dep(2), at_col(j), 1])
    send(("k", 3), T.at[0, stream(3)], T.at[1, stream(3)], sibling)
    for i in (1, 2, 3):
        receive(("k", i), T.at[1, stream(i)])
        enter(i)

    def transpose(c):
        rows = jnp.concatenate(
            [T[0, y, c, half] for half in range(2) for y in range(SIDE)], axis=0
        )
        TT[:, c * 2 * SIDE * SUB : (c + 1) * 2 * SIDE * SUB] = rows.T

    transpose(0)
    transpose(1)
    for i in range(1, 4):
        pass_on(i, 0, 0, 3)
        pass_on(i, 1, 1, -2)
    transpose(2)
    transpose(3)
    for i in range(4):
        pass_on(i, 0, 1, 2)
        pass_on(i, 1, 2, -1)
    for i in range(4):
        pass_on(i, 0, 2, 1)
    for i in range(4):
        finish(i)

    order = (0, -1, 1, -2, 2, -3, 3, 4)

    def block_start(q):
        j = order[q]
        block = ring(j)
        for i in range(4):
            receive(("s", i, -j), G.at[block, 1 - k, stream(i)])

        def tile(n, carry):
            at = pl.multiple_of(n * TILE, TILE)
            total = jnp.zeros((SIDE * SUB, TILE), f32)
            for half in range(2):
                total += lax.dot_general(
                    G[block, half].reshape(SIDE * SUB, HALF), W[half, pl.ds(at, TILE)],
                    (((1,), (1,)), ((), ())), preferred_element_type=f32,
                )
            GT[q, :, :, pl.ds(at, TILE)] = total.reshape(SIDE, SUB, TILE)
            return carry

        lax.fori_loop(0, HALF // TILE, tile, 0)
        y_send[q, 0] = GT[q, at_dep(2)].astype(bf16)
        send(("p", q, 0), y_send.at[q, 0], y_recv.at[q, 0], device(dy=tau))
        y_send[q, 1] = GT[q, at_dep(-1)].astype(bf16)
        send(("p", q, 2), y_send.at[q, 1], y_recv.at[q, 2], device(dy=-tau))

    def block_pass(q):
        receive(("p", q, 0), y_recv.at[q, 0])
        y_recv[q, 0] = (y_recv[q, 0].astype(f32) + GT[q, at_dep(1)]).astype(bf16)
        send(("p", q, 1), y_recv.at[q, 0], y_recv.at[q, 1], device(dy=tau))

    base = number("x")
    for extra in range(1, 2 * SIDE):
        number(("x", extra))

    def x_copy(n, source, target, to):
        return pltpu.make_async_remote_copy(
            src_ref=source, dst_ref=target, send_sem=send_sem.at[base + n],
            recv_sem=recv_sem.at[base + n], device_id=to,
            device_id_type=pl.DeviceIdType.MESH,
        )

    def block_end(q):
        receive(("p", q, 1), y_recv.at[q, 1])
        receive(("p", q, 2), y_recv.at[q, 2])
        total = GT[q, dep] + y_recv[q, 1].astype(f32) + y_recv[q, 2].astype(f32)
        block = ring(order[q])
        half, home = lax.rem(block, 2), block // 2
        away = wrap(home - col, SIDE)

        @pl.when(away == 0)
        def _():
            x_own[half] = total

        @pl.when(away != 0)
        def _():
            x_send[half, away] = total.astype(bf16)
            x_copy(
                half * SIDE + away, x_send.at[half, away], x_recv.at[half, away],
                device(dx=away),
            ).start()

    def grad_weight(begin, end):
        def tile(n, carry):
            half = n // 3
            inner = pl.multiple_of(lax.rem(n, 3) * TILE, TILE)
            right = G[:, half, :, :, pl.ds(inner, TILE)].reshape(RING * SIDE * SUB, TILE)
            total = jnp.dot(TT[...], right, preferred_element_type=f32)
            gw_out[:, pl.ds(pl.multiple_of(n * TILE, TILE), TILE)] = total.astype(bf16)
            return carry

        lax.fori_loop(begin, end, tile, 0)

    for i in range(4):
        relay(i, 1)
    block_start(0)
    for i in range(4):
        relay(i, 2)
    block_pass(0)
    block_start(1)
    block_start(2)
    for i in range(4):
        relay(i, 3)
    block_end(0)
    block_pass(1)
    block_pass(2)
    block_start(3)
    block_start(4)
    for i in range(4):
        relay(i, 4)
    block_end(1)
    block_end(2)
    block_pass(3)
    block_pass(4)
    block_start(5)
    block_start(6)
    block_start(7)
    block_end(3)
    block_end(4)
    block_pass(5)
    block_pass(6)
    grad_weight(0, 2)
    block_pass(7)
    block_end(5)
    block_end(6)
    grad_weight(2, 4)
    block_end(7)
    grad_weight(4, 6)

    for step in range(SIDE):
        for flip in range(2):
            if step or flip:
                core = 1 - k if flip else k
                receive(("a", step, flip), act_recv.at[wrap(dep - step, SIDE), core])
    for piece in range(SIDE):
        for half in range(2):
            begin = piece * CHUNK + half * HALF
            act_out[:, begin : begin + HALF] = (
                act_recv[piece, half].astype(f32)[:SHARE].astype(bf16)
            )

    for half in range(2):
        total = x_own[half]
        for away in range(1, SIDE):
            slot = x_recv.at[half, away]
            x_copy(half * SIDE + away, slot, slot, sibling).wait_recv()
            total += x_recv[half, away].astype(f32)
        gt_out[half] = total.astype(bf16)
    for transfer in pending:
        transfer.wait_send()
    for half in range(2):
        for away in range(1, SIDE):
            slot = x_recv.at[half, away]
            x_copy(half * SIDE + away, slot, slot, sibling).wait_send()


def on_device(tokens, weight, cotangent):
    scratch = [
        pltpu.VMEM((2, SIDE, SIDE, 2, SUB, HALF), bf16),
        pltpu.VMEM((2, HALF, HALF), bf16),
        pltpu.VMEM((HALF, HALF), bf16),
        pltpu.VMEM((SIDE, RING, SUB, HALF), f32),
        pltpu.VMEM((SIDE, 2, 4, SUB, HALF), bf16),
        pltpu.VMEM((SIDE, 2, SUB, HALF), bf16),
        pltpu.VMEM((SIDE, 2, PADDED, HALF), bf16),
        pltpu.VMEM((SIDE, 2, PADDED, HALF), bf16),
        pltpu.VMEM((SIDE, 2, PADDED, HALF), bf16),
        pltpu.VMEM((SIDE, 2, PADDED, HALF), bf16),
        pltpu.VMEM((RING, 2, SIDE, SUB, HALF), bf16),
        pltpu.VMEM((HALF, RING * SIDE * SUB), bf16),
        pltpu.VMEM((RING, SIDE, SUB, HALF), f32),
        pltpu.VMEM((RING, 2, SUB, HALF), bf16),
        pltpu.VMEM((RING, 3, SUB, HALF), bf16),
        pltpu.VMEM((2, SIDE, SUB, HALF), bf16),
        pltpu.VMEM((2, SIDE, SUB, HALF), bf16),
        pltpu.VMEM((2, SUB, HALF), f32),
        pltpu.SemaphoreType.DMA((3,)),
        pltpu.SemaphoreType.DMA((256,)),
        pltpu.SemaphoreType.DMA((256,)),
    ]
    activated, grad_tokens, grad_weight = pl.pallas_call(
        kernel,
        out_shape=(
            jax.ShapeDtypeStruct((SHARE, SIDE * CHUNK), bf16),
            jax.ShapeDtypeStruct((2, SUB, HALF), bf16),
            jax.ShapeDtypeStruct((HALF, CHUNK), bf16),
        ),
        in_specs=[
            pl.BlockSpec(memory_space=pl.ANY),
            pl.BlockSpec(memory_space=pl.ANY),
            pl.BlockSpec(memory_space=pltpu.VMEM),
        ],
        out_specs=[pl.BlockSpec(memory_space=pltpu.VMEM)] * 3,
        scratch_shapes=scratch,
        compiler_params=pltpu.CompilerParams(
            collective_id=0, has_side_effects=True, vmem_limit_bytes=60 * 2**20
        ),
        cost_estimate=pl.CostEstimate(
            flops=11 * 10**9, bytes_accessed=8 * 10**6, transcendentals=10**5
        ),
        name="gelu_grid",
    )(tokens.reshape(2, SUB, HALF), weight, cotangent)
    return activated, grad_tokens.reshape(2 * SUB, HALF), grad_weight


def solution(mesh):
    placed = (P(("depth", "col"), "row"), P("row", "col"), P(("depth", "row"), "col"))
    return jax.shard_map(
        on_device,
        mesh=mesh,
        in_specs=placed,
        out_specs=(
            P(("depth", "row"), "col"),
            P(("depth", "col"), "row"),
            P("row", ("col", "depth")),
        ),
        check_vma=False,
    )
```

```python
import functools
import math

import jax
import jax.numpy as jnp
from jax import lax
from jax.experimental import pallas as pl
from jax.experimental.pallas import tpu as pltpu
from jax.sharding import PartitionSpec as P

root_coef = math.sqrt(2.0 / math.pi)
cubic_coef = 0.044715

RING = 8
SIDE = 4
SUB = 48
HALF = 768
CHUNK = 2 * HALF
SHARE = 24
PADDED = 32
TILE = 256
f32, bf16 = jnp.float32, jnp.bfloat16


def wrap(value, extent):
    return lax.rem(value + 2 * extent, extent)


PIECES = 4


def kernel(
    tok, weight, cot, act_out, gt_out, gw_out,
    T, T_sib, W, W_rest, W_sib, part, hop, first, cot_send, cot_recv, cot_both,
    act_both, act_send, act_recv, g_send, G, TT, GT, y_send, y_recv, x_send, x_recv, x_own,
    gw_tiles, cot_held, act_held, gt_held, local_sem, send_sem, recv_sem,
):
    row, col, dep = (lax.axis_index(name) for name in ("row", "col", "depth"))
    z, k = row // 2, lax.rem(row, 2)
    tau = 1 - 2 * k

    def device(dz=0, dx=0, dy=0, flip=False):
        core = 1 - k if flip else k
        return (2 * wrap(z + dz, RING) + core, wrap(col + dx, SIDE), wrap(dep + dy, SIDE))

    sibling = device(flip=True)
    numbers = {}
    groups = {}

    def number(key):
        return numbers.setdefault(key, len(numbers))

    def copy(group, key, source, target, to):
        return pltpu.make_async_remote_copy(
            src_ref=source, dst_ref=target,
            send_sem=send_sem.at[groups.setdefault(group, len(groups))],
            recv_sem=recv_sem.at[number(key)],
            device_id=to, device_id_type=pl.DeviceIdType.MESH,
        )

    def send(group, key, source, target, to):
        copy(group, key, source, target, to).start()

    def receive(key, size):
        copy("x", key, size, size, sibling).wait_recv()

    def all_sent(group, size):
        copy(group, ("x", 1), size, size, sibling).wait_send()

    def at_col(j):
        return wrap(col + j * tau, SIDE)

    def at_dep(j):
        return wrap(dep + j * tau, SIDE)

    def ring(j):
        return wrap(z + j * tau, RING)

    steps = (0, 2, 1, -1)

    def unit_group(i):
        return wrap(dep + steps[i], SIDE)

    def token_group(i):
        return wrap(dep - steps[i], SIDE)

    def lanes_of(i, half):
        return pl.ds(pl.multiple_of(unit_group(i) * CHUNK + half * HALF, HALF), HALF)

    local = [pltpu.make_async_copy(tok, T.at[dep, col], local_sem.at[0])]
    for i in range(SIDE):
        local.append(
            pltpu.make_async_copy(weight.at[:, lanes_of(i, k)], W.at[i], local_sem.at[1 + i])
        )
    local.append(pltpu.make_async_copy(weight.at[:, lanes_of(0, 1 - k)], W_rest, local_sem.at[5]))
    local.append(pltpu.make_async_copy(cot, cot_held, local_sem.at[6]))
    for transfer in local:
        transfer.start()

    partners = [device(dz=1), device(dz=-1), sibling]
    for step in range(1, SIDE):
        partners += [device(dx=step), device(dy=step)]
    barrier = pltpu.get_barrier_semaphore()
    for partner in partners:
        pl.semaphore_signal(barrier, inc=1, device_id=partner, device_id_type=pl.DeviceIdType.MESH)
    gap = jnp.zeros((PADDED - SHARE, HALF), f32)

    def padded(values):
        return jnp.concatenate([values, gap], axis=0).astype(bf16)

    pl.semaphore_wait(barrier, len(partners))

    for j in (1, -1, 2):
        send("x", ("x", j), tok, T.at[dep, col], device(dx=j * tau))
    send("k", "k", tok, T_sib.at[col], sibling)
    for i in range(SIDE):
        send("w", ("w", i), weight.at[:, lanes_of(i, 1 - k)], W_sib.at[i], sibling)
    for transfer in local:
        transfer.wait()
    for i in range(SIDE):
        cot_send[i] = padded(cot_held[:, lanes_of(i, 1 - k)].astype(f32))
        send("c", "c", cot_send.at[i], cot_recv.at[i], sibling)
    for j in (1, -1, 2):
        slot = T.at[dep, at_col(-j)]
        receive(("x", j), slot)
        send("k", "k" if j != 2 else "k2", slot, T_sib.at[at_col(-j)], sibling)
    for s in (1, -1):
        send("y", "y" if s == 1 else "ys", T.at[dep], T.at[dep], device(dy=s * tau))

    def relay_tokens():
        slot = T.at[at_dep(-1)]
        receive("y", slot)
        send("y", "ys", slot, slot, device(dy=tau))

    def partial_preact(i, columns):
        count = len(columns) * 2 * SUB

        def tile(n, carry):
            lanes = pl.ds(pl.multiple_of(n * TILE, TILE), TILE)
            own = jnp.stack([T[dep, at_col(j)] for j in columns]).reshape(count, HALF)
            other = jnp.stack([T_sib[at_col(j)] for j in columns]).reshape(count, HALF)
            total = jnp.dot(own, W[i, :, lanes], preferred_element_type=f32)
            total += jnp.dot(other, W_sib[i, :, lanes], preferred_element_type=f32)
            total = total.reshape(len(columns), 2, SUB, TILE)
            for n, j in enumerate(columns):
                part[i, at_col(j), :, :, lanes] = total[n]
            return carry

        lax.fori_loop(0, HALF // TILE, tile, 0)

    def of_block(i, block):
        return part[i, block // 2, lax.rem(block, 2)]

    def enter(i):
        first[i, 0] = of_block(i, ring(4)).astype(bf16)
        send("r", ("r", i, 1), first.at[i, 0], hop.at[i, 0], device(dz=tau))
        first[i, 1] = of_block(i, ring(-3)).astype(bf16)
        send("r", ("r", i, 1), first.at[i, 1], hop.at[i, 4], device(dz=-tau))

    def reduce_step(i, at):
        receive(("r", i, at), hop.at[i, pl.ds(0, 2 if at < 3 else 1)])
        for way in range(2 if at < 3 else 1):
            slot, j = (at - 1, 4 - at) if way == 0 else (3 + at, at - 3)
            later = 4 if slot + 1 in (3, 6) else at + 1
            hop[i, slot] = (hop[i, slot].astype(f32) + of_block(i, ring(j))).astype(bf16)
            send(
                "r", ("r", i, later), hop.at[i, slot], hop.at[i, slot + 1],
                device(dz=tau if way == 0 else -tau),
            )

    def spread(i, block, ways):
        slot = G.at[block, k, token_group(i)]
        for group, key, to in ways:
            send(group, key, slot, slot, to)

    def share(i, far):
        if far == 0:
            return ("s", 0)
        if far == 4:
            return ("s", 4, i)
        return ("s", far, (2, 0, 1, 1)[i])

    def begin(i):
        if i > 0:
            receive(("h", i), G.at[z, k, token_group(i)])
        spread(i, z, [
            ("g", ("g", i, 1), device(dz=tau)), ("g", ("g", i, 1), device(dz=-tau)),
            ("s", share(i, 0), sibling),
        ])

    def finish(i):
        receive(("r", i, 4), hop.at[i, pl.ds(0, 2)])
        v = of_block(i, z) + hop[i, 3].astype(f32) + hop[i, 6].astype(f32)
        cot_both[k] = cot_held[:, lanes_of(i, k)].astype(f32)
        cot_both[1 - k] = cot_recv[i].astype(f32)[:SHARE]
        given = cot_both[...].reshape(SUB, HALF)
        hyper = jnp.tanh(root_coef * (v + cubic_coef * v * v * v))
        inner = root_coef * (1.0 + 3.0 * cubic_coef * v * v)
        slope = 0.5 * (1.0 + hyper) + 0.5 * v * (1.0 - hyper * hyper) * inner
        gradient = (given * slope).astype(bf16)
        if i == 0:
            G[z, k, dep] = gradient
            begin(0)
        else:
            g_send[i] = gradient
            send("h", ("h", i), g_send.at[i], G.at[z, k, dep], device(dy=steps[i]))
        act_both[...] = (0.5 * v * (1.0 + hyper)).reshape(2, SHARE, HALF)
        act_held[:, lanes_of(i, k)] = act_both[k].astype(bf16)
        act_send[i] = padded(act_both[1 - k])
        send("a", "a", act_send.at[i], act_recv.at[i], sibling)

    def relay(i, far):
        receive(("g", i, far), hop.at[0, pl.ds(0, 2 if far < 4 else 1)])
        for way in range(2 if far < 4 else 1):
            ways = []
            if far < (4 if way == 0 else 3):
                ways.append(("g", ("g", i, far + 1), device(dz=tau if way == 0 else -tau)))
            ways.append(("s", share(i, far), sibling))
            spread(i, ring(-far if way == 0 else far), ways)

    def transpose(y):
        rows = T[y].reshape(RING * SUB, HALF)
        TT[:, y * RING * SUB : (y + 1) * RING * SUB] = rows.T

    def blocks(far):
        if far == 0:
            return [(0, z)]
        if far == 4:
            return [(7, ring(4))]
        return [(2 * far - 1, ring(-far)), (2 * far, ring(far))]

    def partial_tokens(far, streams):
        pieces = [(q, block, token_group(i)) for i in streams for q, block in blocks(far)]
        receive(share(streams[0], far), hop.at[0, pl.ds(0, len(pieces))])

        def tile(n, carry):
            at = pl.multiple_of(n * TILE, TILE)
            total = jnp.zeros((len(pieces) * SUB, TILE), f32)
            for half, right in ((k, W.at[0]), (1 - k, W_rest)):
                left = jnp.concatenate([G[block, half, group] for q, block, group in pieces], axis=0)
                total += lax.dot_general(
                    left, right[pl.ds(at, TILE)], (((1,), (1,)), ((), ())),
                    preferred_element_type=f32,
                )
            for m, (q, block, group) in enumerate(pieces):
                GT[q, group, :, pl.ds(at, TILE)] = total[m * SUB : (m + 1) * SUB]
            return carry

        lax.fori_loop(0, HALF // TILE, tile, 0)

    def send_piece(far, key, q, n, j, to):
        y_send[q, n] = GT[q, at_dep(j)].astype(bf16)
        send("p", key, y_send.at[q, n], y_recv.at[q, n], device(dy=to * tau))

    def stage_far_row(far):
        for q, block in blocks(far):
            send_piece(far, ("p", far, 0), q, 0, 2, 1)

    def stage_near_row(far):
        for q, block in blocks(far):
            send_piece(far, ("p", far, 1), q, 2, -1, -1)

    def block_one(far):
        partial_tokens(far, (1,))
        stage_far_row(far)

    def block_two(far):
        partial_tokens(far, (2, 3))
        stage_near_row(far)

    def block_pass(far):
        receive(("p", far, 0), hop.at[0, pl.ds(0, len(blocks(far)))])
        for q, block in blocks(far):
            y_recv[q, 0] = (y_recv[q, 0].astype(f32) + GT[q, at_dep(1)]).astype(bf16)
            send("p", ("p", far, 1), y_recv.at[q, 0], y_recv.at[q, 1], device(dy=tau))

    def last_block(i):
        partial_tokens(4, (i,))
        if i > 0:
            y_send[7, i - 1] = GT[7, token_group(i)].astype(bf16)
            send(
                "p", ("p", 4), y_send.at[7, i - 1], y_recv.at[7, i - 1], device(dy=-steps[i])
            )

    def block_end(far):
        key = ("p", 4) if far == 4 else ("p", far, 1)
        receive(key, hop.at[0, pl.ds(0, 3 if far == 4 else 2 * len(blocks(far)))])
        for q, block in blocks(far):
            total = GT[q, dep]
            for n in range(0 if far == 4 else 1, 3):
                total += y_recv[q, n].astype(f32)
            half, home = lax.rem(block, 2), block // 2
            away = wrap(home - col, SIDE)

            @pl.when(away == 0)
            def _():
                x_own[half] = total

            @pl.when(away != 0)
            def _():
                x_send[half, away - 1] = total.astype(bf16)
                send(
                    "home", "home", x_send.at[half, away - 1], x_recv.at[half, away - 1],
                    device(dx=away),
                )

    def write_tile(n):
        return pltpu.make_async_copy(
            gw_tiles.at[n], gw_out.at[:, pl.ds(pl.multiple_of(n * TILE, TILE), TILE)],
            local_sem.at[n],
        )

    def grad_weight(begin, end):
        def tile(n, carry):
            half = n // 3
            inner = pl.multiple_of(lax.rem(n, 3) * TILE, TILE)
            right = jnp.concatenate(
                [G[:, half, y, :, pl.ds(inner, TILE)].reshape(RING * SUB, TILE) for y in range(4)],
                axis=0,
            )
            gw_tiles[n] = jnp.dot(TT[...], right, preferred_element_type=f32).astype(bf16)
            write_tile(n).start()
            return carry

        lax.fori_loop(begin, end, tile, 0)

    write_act = pltpu.make_async_copy(act_held, act_out, local_sem.at[6])
    write_gt = pltpu.make_async_copy(gt_held, gt_out, local_sem.at[7])

    def activations():
        receive("a", act_recv)
        for i in range(SIDE):
            act_held[:, lanes_of(i, 1 - k)] = act_recv[i].astype(f32)[:SHARE].astype(bf16)
        write_act.start()

    turns = (1, 2, 3, 0)

    receive("k", T.at[0, pl.ds(0, 3)])
    receive(("w", turns[0]), W_sib.at[turns[0]])
    partial_preact(turns[0], (0, 1, -1))
    receive("k2", T.at[0, 0])
    partial_preact(turns[0], (2,))
    enter(turns[0])
    for i in turns[1:]:
        receive(("w", i), W_sib.at[i])
        partial_preact(i, (0, 1, -1, 2))
        enter(i)
    for i in turns:
        reduce_step(i, 1)
    relay_tokens()
    for at in (2, 3):
        for i in turns:
            reduce_step(i, at)
    receive("c", cot_recv)
    for i in turns:
        finish(i)
    for i in (1, 2, 3):
        begin(i)
    receive("ys", T.at[pl.ds(0, 2)])
    partial_tokens(0, (0, 1, 2, 3))
    stage_far_row(0)
    stage_near_row(0)
    for far in (1, 2, 3):
        relay(1, far)
        block_pass(far - 1)
        if far > 1:
            partial_tokens(far - 1, (0,))
        relay(2, far)
        block_one(far)
        relay(3, far)
        if far == 1:
            transpose(0)
            transpose(1)
        if far == 2:
            transpose(2)
            transpose(3)
        if far == 3:
            activations()
        relay(0, far)
        block_two(far)
        block_end(far - 1)
    relay(1, 4)
    block_pass(3)
    relay(2, 4)
    last_block(1)
    relay(3, 4)
    last_block(2)
    relay(0, 4)
    last_block(3)
    partial_tokens(3, (0,))
    last_block(0)
    grad_weight(0, 1)
    block_end(3)
    grad_weight(1, 3)
    block_end(4)
    grad_weight(3, 6)

    receive("home", hop.at[0, pl.ds(0, 6)])
    for half in range(2):
        total = x_own[half]
        for n in range(SIDE - 1):
            total += x_recv[half, n].astype(f32)
        gt_held[half] = total.astype(bf16)
    write_gt.start()
    for group, size in (
        ("x", T.at[0, pl.ds(0, 3)]), ("k", T.at[0]), ("w", W_sib), ("c", cot_recv),
        ("y", T.at[pl.ds(0, 3)]), ("r", hop), ("h", g_send.at[pl.ds(0, 3)]), ("g", hop),
        ("s", G.at[pl.ds(0, 4)]), ("a", act_recv), ("p", y_recv), ("home", x_send),
    ):
        all_sent(group, size)
    for n in range(CHUNK // TILE):
        write_tile(n).wait()
    write_act.wait()
    write_gt.wait()


def deliver(act, gt, gw, act_out, gt_out, gw_out, act_held, gt_held, gw_held, sem):
    moves = [(act, act_held, act_out), (gt, gt_held, gt_out)]
    for n in range(PIECES):
        rows = pl.ds(n * (HALF // PIECES), HALF // PIECES)
        moves.append((gw.at[rows], gw_held.at[rows], gw_out.at[rows]))
    into = [
        pltpu.make_async_copy(source, held, sem.at[0, n])
        for n, (source, held, target) in enumerate(moves)
    ]
    out_of = [
        pltpu.make_async_copy(held, target, sem.at[1, n])
        for n, (source, held, target) in enumerate(moves)
    ]
    for move in into:
        move.start()
    for arrived, move in zip(into, out_of):
        arrived.wait()
        move.start()
    for move in out_of:
        move.wait()


def on_device(tokens, weight, cotangent):
    scratch = [
        pltpu.VMEM((SIDE, SIDE, 2, SUB, HALF), bf16),
        pltpu.VMEM((SIDE, 2, SUB, HALF), bf16),
        pltpu.VMEM((SIDE, HALF, HALF), bf16),
        pltpu.VMEM((HALF, HALF), bf16),
        pltpu.VMEM((SIDE, HALF, HALF), bf16),
        pltpu.VMEM((SIDE, SIDE, 2, SUB, HALF), f32),
        pltpu.VMEM((SIDE, 7, SUB, HALF), bf16),
        pltpu.VMEM((SIDE, 2, SUB, HALF), bf16),
        pltpu.VMEM((SIDE, PADDED, HALF), bf16),
        pltpu.VMEM((SIDE, PADDED, HALF), bf16),
        pltpu.VMEM((2, SHARE, HALF), f32),
        pltpu.VMEM((2, SHARE, HALF), f32),
        pltpu.VMEM((SIDE, PADDED, HALF), bf16),
        pltpu.VMEM((SIDE, PADDED, HALF), bf16),
        pltpu.VMEM((SIDE, SUB, HALF), bf16),
        pltpu.VMEM((RING, 2, SIDE, SUB, HALF), bf16),
        pltpu.VMEM((HALF, RING * SIDE * SUB), bf16),
        pltpu.VMEM((RING, SIDE, SUB, HALF), f32),
        pltpu.VMEM((RING, 3, SUB, HALF), bf16),
        pltpu.VMEM((RING, 3, SUB, HALF), bf16),
        pltpu.VMEM((2, SIDE - 1, SUB, HALF), bf16),
        pltpu.VMEM((2, SIDE - 1, SUB, HALF), bf16),
        pltpu.VMEM((2, SUB, HALF), f32),
        pltpu.VMEM((CHUNK // TILE, HALF, TILE), bf16),
        pltpu.VMEM((SHARE, SIDE * CHUNK), bf16),
        pltpu.VMEM((SHARE, SIDE * CHUNK), bf16),
        pltpu.VMEM((2, SUB, HALF), bf16),
        pltpu.SemaphoreType.DMA((8,)),
        pltpu.SemaphoreType.DMA((12,)),
        pltpu.SemaphoreType.DMA((72,)),
    ]
    out_shape = (
        jax.ShapeDtypeStruct((SHARE, SIDE * CHUNK), bf16),
        jax.ShapeDtypeStruct((2, SUB, HALF), bf16),
        jax.ShapeDtypeStruct((HALF, CHUNK), bf16),
    )
    anywhere = pl.BlockSpec(memory_space=pl.ANY)
    results = pl.pallas_call(
        kernel,
        out_shape=out_shape,
        in_specs=[anywhere] * 3,
        out_specs=[anywhere] * 3,
        scratch_shapes=scratch,
        compiler_params=pltpu.CompilerParams(
            collective_id=0, has_side_effects=True, vmem_limit_bytes=60 * 2**20
        ),
        cost_estimate=pl.CostEstimate(
            flops=11 * 10**9, bytes_accessed=15 * 10**6, transcendentals=10**5
        ),
        name="gelu_grid",
    )(tokens.reshape(2, SUB, HALF), weight, cotangent)
    activated, grad_tokens, grad_weight = pl.pallas_call(
        deliver,
        out_shape=out_shape,
        in_specs=[anywhere] * 3,
        out_specs=[anywhere] * 3,
        scratch_shapes=[pltpu.VMEM(shape.shape, bf16) for shape in out_shape]
        + [pltpu.SemaphoreType.DMA((2, PIECES + 2))],
        name="deliver",
    )(*results)
    return activated, grad_tokens.reshape(2 * SUB, HALF), grad_weight


def solution(mesh):
    placed = (P(("depth", "col"), "row"), P("row", "col"), P(("depth", "row"), "col"))
    return jax.shard_map(
        on_device,
        mesh=mesh,
        in_specs=placed,
        out_specs=(
            P(("depth", "row"), "col"),
            P(("depth", "col"), "row"),
            P("row", ("col", "depth")),
        ),
        check_vma=False,
    )
```

```python
import functools
import math

import jax
import jax.numpy as jnp
from jax import lax
from jax.experimental import pallas as pl
from jax.experimental.pallas import tpu as pltpu
from jax.sharding import PartitionSpec as P

root_coef = math.sqrt(2.0 / math.pi)
cubic_coef = 0.044715

RING = 8
SIDE = 4
SUB = 48
HALF = 768
CHUNK = 2 * HALF
SHARE = 24
PADDED = 32
TILE = 256
f32, bf16 = jnp.float32, jnp.bfloat16


def wrap(value, extent):
    return lax.rem(value + 2 * extent, extent)


PIECES = 8


def kernel(
    tok, weight, cot, act_out, gt_out, gw_out,
    T, T_sib, W, W_rest, W_sib, part, hop, first, cot_send, cot_recv, cot_both,
    act_both, act_send, act_recv, g_send, G, TT, GT, y_send, y_recv, x_send, x_recv, x_own,
    gw_tiles, cot_held, act_held, gt_held, local_sem, send_sem, recv_sem,
):
    row, col, dep = (lax.axis_index(name) for name in ("row", "col", "depth"))
    z, k = row // 2, lax.rem(row, 2)
    tau = 1 - 2 * k

    def device(dz=0, dx=0, dy=0, flip=False):
        core = 1 - k if flip else k
        return (2 * wrap(z + dz, RING) + core, wrap(col + dx, SIDE), wrap(dep + dy, SIDE))

    sibling = device(flip=True)
    numbers = {}
    groups = {}

    def number(key):
        return numbers.setdefault(key, len(numbers))

    def copy(group, key, source, target, to):
        return pltpu.make_async_remote_copy(
            src_ref=source, dst_ref=target,
            send_sem=send_sem.at[groups.setdefault(group, len(groups))],
            recv_sem=recv_sem.at[number(key)],
            device_id=to, device_id_type=pl.DeviceIdType.MESH,
        )

    def send(group, key, source, target, to):
        copy(group, key, source, target, to).start()

    def receive(key, size):
        copy("x", key, size, size, sibling).wait_recv()

    def all_sent(group, size):
        copy(group, ("x", 1), size, size, sibling).wait_send()

    def at_col(j):
        return wrap(col + j * tau, SIDE)

    def at_dep(j):
        return wrap(dep + j * tau, SIDE)

    def ring(j):
        return wrap(z + j * tau, RING)

    steps = (0, 2, 1, -1)

    def unit_group(i):
        return wrap(dep + steps[i], SIDE)

    def token_group(i):
        return wrap(dep - steps[i], SIDE)

    def lanes_of(i, half):
        return pl.ds(pl.multiple_of(unit_group(i) * CHUNK + half * HALF, HALF), HALF)

    local = [pltpu.make_async_copy(tok, T.at[dep, col], local_sem.at[0])]
    for i in range(SIDE):
        local.append(
            pltpu.make_async_copy(weight.at[:, lanes_of(i, k)], W.at[i], local_sem.at[1 + i])
        )
    local.append(pltpu.make_async_copy(weight.at[:, lanes_of(0, 1 - k)], W_rest, local_sem.at[5]))
    local.append(pltpu.make_async_copy(cot, cot_held, local_sem.at[6]))
    for transfer in local:
        transfer.start()

    partners = [device(dz=1), device(dz=-1), sibling]
    for step in range(1, SIDE):
        partners += [device(dx=step), device(dy=step)]
    barrier = pltpu.get_barrier_semaphore()
    for partner in partners:
        pl.semaphore_signal(barrier, inc=1, device_id=partner, device_id_type=pl.DeviceIdType.MESH)
    gap = jnp.zeros((PADDED - SHARE, HALF), f32)

    def padded(values):
        return jnp.concatenate([values, gap], axis=0).astype(bf16)

    pl.semaphore_wait(barrier, len(partners))

    for j in (1, -1, 2):
        send("x", ("x", j), tok, T.at[dep, col], device(dx=j * tau))
    send("k", "k", tok, T_sib.at[col], sibling)
    for i in range(SIDE):
        send("w", ("w", i), weight.at[:, lanes_of(i, 1 - k)], W_sib.at[i], sibling)
    for transfer in local:
        transfer.wait()
    for i in range(SIDE):
        cot_send[i] = padded(cot_held[:, lanes_of(i, 1 - k)].astype(f32))
        send("c", "c", cot_send.at[i], cot_recv.at[i], sibling)
    for j in (1, -1, 2):
        slot = T.at[dep, at_col(-j)]
        receive(("x", j), slot)
        send("k", "k" if j != 2 else "k2", slot, T_sib.at[at_col(-j)], sibling)
    for s in (1, -1):
        send("y", "y" if s == 1 else "ys", T.at[dep], T.at[dep], device(dy=s * tau))

    def relay_tokens():
        slot = T.at[at_dep(-1)]
        receive("y", slot)
        send("y", "ys", slot, slot, device(dy=tau))

    def partial_preact(i, columns):
        count = len(columns) * 2 * SUB

        def tile(n, carry):
            lanes = pl.ds(pl.multiple_of(n * TILE, TILE), TILE)
            own = jnp.stack([T[dep, at_col(j)] for j in columns]).reshape(count, HALF)
            other = jnp.stack([T_sib[at_col(j)] for j in columns]).reshape(count, HALF)
            total = jnp.dot(own, W[i, :, lanes], preferred_element_type=f32)
            total += jnp.dot(other, W_sib[i, :, lanes], preferred_element_type=f32)
            total = total.reshape(len(columns), 2, SUB, TILE)
            for n, j in enumerate(columns):
                part[i, at_col(j), :, :, lanes] = total[n]
            return carry

        lax.fori_loop(0, HALF // TILE, tile, 0)

    def of_block(i, block):
        return part[i, block // 2, lax.rem(block, 2)]

    def enter(i):
        first[i, 0] = of_block(i, ring(4)).astype(bf16)
        send("r", ("r", i, 1), first.at[i, 0], hop.at[i, 0], device(dz=tau))
        first[i, 1] = of_block(i, ring(-3)).astype(bf16)
        send("r", ("r", i, 1), first.at[i, 1], hop.at[i, 4], device(dz=-tau))

    def reduce_step(i, at):
        receive(("r", i, at), hop.at[i, pl.ds(0, 2 if at < 3 else 1)])
        for way in range(2 if at < 3 else 1):
            slot, j = (at - 1, 4 - at) if way == 0 else (3 + at, at - 3)
            later = 4 if slot + 1 in (3, 6) else at + 1
            hop[i, slot] = (hop[i, slot].astype(f32) + of_block(i, ring(j))).astype(bf16)
            send(
                "r", ("r", i, later), hop.at[i, slot], hop.at[i, slot + 1],
                device(dz=tau if way == 0 else -tau),
            )

    def spread(i, block, ways):
        slot = G.at[block, k, token_group(i)]
        for group, key, to in ways:
            send(group, key, slot, slot, to)

    def share(i, far):
        if far == 0:
            return ("s", 0)
        if far == 4:
            return ("s", 4, i)
        return ("s", far, (2, 0, 1, 1)[i])

    def begin(i):
        if i > 0:
            receive(("h", i), G.at[z, k, token_group(i)])
        spread(i, z, [
            ("g", ("g", i, 1), device(dz=tau)), ("g", ("g", i, 1), device(dz=-tau)),
            ("s", share(i, 0), sibling),
        ])

    def finish(i):
        receive(("r", i, 4), hop.at[i, pl.ds(0, 2)])
        v = of_block(i, z) + hop[i, 3].astype(f32) + hop[i, 6].astype(f32)
        cot_both[k] = cot_held[:, lanes_of(i, k)].astype(f32)
        cot_both[1 - k] = cot_recv[i].astype(f32)[:SHARE]
        given = cot_both[...].reshape(SUB, HALF)
        hyper = jnp.tanh(root_coef * (v + cubic_coef * v * v * v))
        inner = root_coef * (1.0 + 3.0 * cubic_coef * v * v)
        slope = 0.5 * (1.0 + hyper) + 0.5 * v * (1.0 - hyper * hyper) * inner
        gradient = (given * slope).astype(bf16)
        if i == 0:
            G[z, k, dep] = gradient
            begin(0)
        else:
            g_send[i] = gradient
            send("h", ("h", i), g_send.at[i], G.at[z, k, dep], device(dy=steps[i]))
        act_both[...] = (0.5 * v * (1.0 + hyper)).reshape(2, SHARE, HALF)
        act_held[:, lanes_of(i, k)] = act_both[k].astype(bf16)
        act_send[i] = padded(act_both[1 - k])
        send("a", "a", act_send.at[i], act_recv.at[i], sibling)

    def relay(i, far):
        receive(("g", i, far), hop.at[0, pl.ds(0, 2 if far < 4 else 1)])
        for way in range(2 if far < 4 else 1):
            ways = []
            if far < (4 if way == 0 else 3):
                ways.append(("g", ("g", i, far + 1), device(dz=tau if way == 0 else -tau)))
            ways.append(("s", share(i, far), sibling))
            spread(i, ring(-far if way == 0 else far), ways)

    def transpose(y):
        rows = T[y].reshape(RING * SUB, HALF)
        TT[:, y * RING * SUB : (y + 1) * RING * SUB] = rows.T

    def blocks(far):
        if far == 0:
            return [(0, z)]
        if far == 4:
            return [(7, ring(4))]
        return [(2 * far - 1, ring(-far)), (2 * far, ring(far))]

    def partial_tokens(far, streams):
        pieces = [(q, block, token_group(i)) for i in streams for q, block in blocks(far)]
        receive(share(streams[0], far), hop.at[0, pl.ds(0, len(pieces))])

        def tile(n, carry):
            at = pl.multiple_of(n * TILE, TILE)
            total = jnp.zeros((len(pieces) * SUB, TILE), f32)
            for half, right in ((k, W.at[0]), (1 - k, W_rest)):
                left = jnp.concatenate([G[block, half, group] for q, block, group in pieces], axis=0)
                total += lax.dot_general(
                    left, right[pl.ds(at, TILE)], (((1,), (1,)), ((), ())),
                    preferred_element_type=f32,
                )
            for m, (q, block, group) in enumerate(pieces):
                GT[q, group, :, pl.ds(at, TILE)] = total[m * SUB : (m + 1) * SUB]
            return carry

        lax.fori_loop(0, HALF // TILE, tile, 0)

    def send_piece(far, key, q, n, j, to):
        y_send[q, n] = GT[q, at_dep(j)].astype(bf16)
        send("p", key, y_send.at[q, n], y_recv.at[q, n], device(dy=to * tau))

    def stage_far_row(far):
        for q, block in blocks(far):
            send_piece(far, ("p", far, 0), q, 0, 2, 1)

    def stage_near_row(far):
        for q, block in blocks(far):
            send_piece(far, ("p", far, 1), q, 2, -1, -1)

    def block_one(far):
        partial_tokens(far, (1,))
        stage_far_row(far)

    def block_two(far):
        partial_tokens(far, (2, 3))
        stage_near_row(far)

    def block_pass(far):
        receive(("p", far, 0), hop.at[0, pl.ds(0, len(blocks(far)))])
        for q, block in blocks(far):
            y_recv[q, 0] = (y_recv[q, 0].astype(f32) + GT[q, at_dep(1)]).astype(bf16)
            send("p", ("p", far, 1), y_recv.at[q, 0], y_recv.at[q, 1], device(dy=tau))

    def last_block(i):
        partial_tokens(4, (i,))
        if i > 0:
            y_send[7, i - 1] = GT[7, token_group(i)].astype(bf16)
            send(
                "p", ("p", 4), y_send.at[7, i - 1], y_recv.at[7, i - 1], device(dy=-steps[i])
            )

    def block_end(far):
        key = ("p", 4) if far == 4 else ("p", far, 1)
        receive(key, hop.at[0, pl.ds(0, 3 if far == 4 else 2 * len(blocks(far)))])
        for q, block in blocks(far):
            total = GT[q, dep]
            for n in range(0 if far == 4 else 1, 3):
                total += y_recv[q, n].astype(f32)
            half, home = lax.rem(block, 2), block // 2
            away = wrap(home - col, SIDE)

            @pl.when(away == 0)
            def _():
                x_own[half] = total

            @pl.when(away != 0)
            def _():
                x_send[half, away - 1] = total.astype(bf16)
                send(
                    "home", "home", x_send.at[half, away - 1], x_recv.at[half, away - 1],
                    device(dx=away),
                )

    def write_tile(n):
        return pltpu.make_async_copy(
            gw_tiles.at[n], gw_out.at[:, pl.ds(pl.multiple_of(n * TILE, TILE), TILE)],
            local_sem.at[n],
        )

    def grad_weight(begin, end):
        def tile(n, carry):
            half = n // 3
            inner = pl.multiple_of(lax.rem(n, 3) * TILE, TILE)
            right = jnp.concatenate(
                [G[:, half, y, :, pl.ds(inner, TILE)].reshape(RING * SUB, TILE) for y in range(4)],
                axis=0,
            )
            gw_tiles[n] = jnp.dot(TT[...], right, preferred_element_type=f32).astype(bf16)
            write_tile(n).start()
            return carry

        lax.fori_loop(begin, end, tile, 0)

    write_act = pltpu.make_async_copy(act_held, act_out, local_sem.at[6])
    write_gt = pltpu.make_async_copy(gt_held, gt_out, local_sem.at[7])

    def activations():
        receive("a", act_recv)
        for i in range(SIDE):
            act_held[:, lanes_of(i, 1 - k)] = act_recv[i].astype(f32)[:SHARE].astype(bf16)
        write_act.start()

    turns = (1, 2, 3, 0)

    receive("k", T.at[0, pl.ds(0, 3)])
    receive(("w", turns[0]), W_sib.at[turns[0]])
    partial_preact(turns[0], (0, 1, -1))
    receive("k2", T.at[0, 0])
    partial_preact(turns[0], (2,))
    enter(turns[0])
    for i in turns[1:]:
        receive(("w", i), W_sib.at[i])
        partial_preact(i, (0, 1, -1, 2))
        enter(i)
    for i, at in ((1, 1), (2, 1), (3, 1), (1, 2), (0, 1)):
        reduce_step(i, at)
    relay_tokens()
    for i, at in ((2, 2), (3, 2), (1, 3), (0, 2), (2, 3), (3, 3)):
        reduce_step(i, at)
    receive("c", cot_recv)
    finish(1)
    reduce_step(0, 3)
    for i in (2, 3, 0):
        finish(i)
    for i in (1, 2, 3):
        begin(i)
    receive("ys", T.at[pl.ds(0, 2)])
    partial_tokens(0, (0, 1, 2, 3))
    stage_far_row(0)
    stage_near_row(0)
    for far in (1, 2, 3):
        relay(1, far)
        if far > 1:
            relay(0, far - 1)
        block_pass(far - 1)
        relay(2, far)
        block_one(far)
        relay(3, far)
        if far > 1:
            partial_tokens(far - 1, (0,))
        if far == 1:
            transpose(0)
            transpose(1)
        if far == 2:
            transpose(2)
            transpose(3)
        if far == 3:
            activations()
        block_two(far)
        block_end(far - 1)
    relay(1, 4)
    relay(0, 3)
    block_pass(3)
    relay(2, 4)
    last_block(1)
    relay(3, 4)
    last_block(2)
    last_block(3)
    partial_tokens(3, (0,))
    relay(0, 4)
    block_end(3)
    last_block(0)
    grad_weight(0, 2)
    block_end(4)
    grad_weight(2, 6)

    receive("home", hop.at[0, pl.ds(0, 6)])
    for half in range(2):
        total = x_own[half]
        for n in range(SIDE - 1):
            total += x_recv[half, n].astype(f32)
        gt_held[half] = total.astype(bf16)
    write_gt.start()
    for group, size in (
        ("x", T.at[0, pl.ds(0, 3)]), ("k", T.at[0]), ("w", W_sib), ("c", cot_recv),
        ("y", T.at[pl.ds(0, 3)]), ("r", hop), ("h", g_send.at[pl.ds(0, 3)]), ("g", hop),
        ("s", G.at[pl.ds(0, 4)]), ("a", act_recv), ("p", y_recv), ("home", x_send),
    ):
        all_sent(group, size)
    for n in range(CHUNK // TILE):
        write_tile(n).wait()
    write_act.wait()
    write_gt.wait()


def deliver(act, gt, gw, act_out, gt_out, gw_out, act_held, gt_held, gw_held, sem):
    moves = [(act, act_held, act_out), (gt, gt_held, gt_out)]
    for n in range(PIECES):
        rows = pl.ds(n * (HALF // PIECES), HALF // PIECES)
        moves.append((gw.at[rows], gw_held.at[rows], gw_out.at[rows]))
    into = [
        pltpu.make_async_copy(source, held, sem.at[0, n])
        for n, (source, held, target) in enumerate(moves)
    ]
    out_of = [
        pltpu.make_async_copy(held, target, sem.at[1, n])
        for n, (source, held, target) in enumerate(moves)
    ]
    for move in into:
        move.start()
    for arrived, move in zip(into, out_of):
        arrived.wait()
        move.start()
    for move in out_of:
        move.wait()


def on_device(tokens, weight, cotangent):
    scratch = [
        pltpu.VMEM((SIDE, SIDE, 2, SUB, HALF), bf16),
        pltpu.VMEM((SIDE, 2, SUB, HALF), bf16),
        pltpu.VMEM((SIDE, HALF, HALF), bf16),
        pltpu.VMEM((HALF, HALF), bf16),
        pltpu.VMEM((SIDE, HALF, HALF), bf16),
        pltpu.VMEM((SIDE, SIDE, 2, SUB, HALF), f32),
        pltpu.VMEM((SIDE, 7, SUB, HALF), bf16),
        pltpu.VMEM((SIDE, 2, SUB, HALF), bf16),
        pltpu.VMEM((SIDE, PADDED, HALF), bf16),
        pltpu.VMEM((SIDE, PADDED, HALF), bf16),
        pltpu.VMEM((2, SHARE, HALF), f32),
        pltpu.VMEM((2, SHARE, HALF), f32),
        pltpu.VMEM((SIDE, PADDED, HALF), bf16),
        pltpu.VMEM((SIDE, PADDED, HALF), bf16),
        pltpu.VMEM((SIDE, SUB, HALF), bf16),
        pltpu.VMEM((RING, 2, SIDE, SUB, HALF), bf16),
        pltpu.VMEM((HALF, RING * SIDE * SUB), bf16),
        pltpu.VMEM((RING, SIDE, SUB, HALF), f32),
        pltpu.VMEM((RING, 3, SUB, HALF), bf16),
        pltpu.VMEM((RING, 3, SUB, HALF), bf16),
        pltpu.VMEM((2, SIDE - 1, SUB, HALF), bf16),
        pltpu.VMEM((2, SIDE - 1, SUB, HALF), bf16),
        pltpu.VMEM((2, SUB, HALF), f32),
        pltpu.VMEM((CHUNK // TILE, HALF, TILE), bf16),
        pltpu.VMEM((SHARE, SIDE * CHUNK), bf16),
        pltpu.VMEM((SHARE, SIDE * CHUNK), bf16),
        pltpu.VMEM((2, SUB, HALF), bf16),
        pltpu.SemaphoreType.DMA((8,)),
        pltpu.SemaphoreType.DMA((12,)),
        pltpu.SemaphoreType.DMA((72,)),
    ]
    out_shape = (
        jax.ShapeDtypeStruct((SHARE, SIDE * CHUNK), bf16),
        jax.ShapeDtypeStruct((2, SUB, HALF), bf16),
        jax.ShapeDtypeStruct((HALF, CHUNK), bf16),
    )
    anywhere = pl.BlockSpec(memory_space=pl.ANY)
    results = pl.pallas_call(
        kernel,
        out_shape=out_shape,
        in_specs=[anywhere] * 3,
        out_specs=[anywhere] * 3,
        scratch_shapes=scratch,
        compiler_params=pltpu.CompilerParams(
            collective_id=0, has_side_effects=True, vmem_limit_bytes=60 * 2**20
        ),
        cost_estimate=pl.CostEstimate(
            flops=11 * 10**9, bytes_accessed=15 * 10**6, transcendentals=10**5
        ),
        name="gelu_grid",
    )(tokens.reshape(2, SUB, HALF), weight, cotangent)
    activated, grad_tokens, grad_weight = pl.pallas_call(
        deliver,
        out_shape=out_shape,
        in_specs=[anywhere] * 3,
        out_specs=[anywhere] * 3,
        scratch_shapes=[pltpu.VMEM(shape.shape, bf16) for shape in out_shape]
        + [pltpu.SemaphoreType.DMA((2, PIECES + 2))],
        name="deliver",
    )(*results)
    return activated, grad_tokens.reshape(2 * SUB, HALF), grad_weight


def solution(mesh):
    placed = (P(("depth", "col"), "row"), P("row", "col"), P(("depth", "row"), "col"))
    return jax.shard_map(
        on_device,
        mesh=mesh,
        in_specs=placed,
        out_specs=(
            P(("depth", "row"), "col"),
            P(("depth", "col"), "row"),
            P("row", ("col", "depth")),
        ),
        check_vma=False,
    )
```

```python
import functools
import math

import jax
import jax.numpy as jnp
from jax import lax
from jax.experimental import pallas as pl
from jax.experimental.pallas import tpu as pltpu
from jax.sharding import PartitionSpec as P

root_coef = math.sqrt(2.0 / math.pi)
cubic_coef = 0.044715

RING = 8
SIDE = 4
SUB = 48
HALF = 768
CHUNK = 2 * HALF
SHARE = 24
PADDED = 32
TILE = 256
f32, bf16 = jnp.float32, jnp.bfloat16


def wrap(value, extent):
    return lax.rem(value + 2 * extent, extent)


PIECES = 8


def kernel(
    tok, weight, cot, act_out, gt_out, gw_out,
    T, T_sib, W, W_rest, W_sib, part, hop, first, cot_send, cot_recv, cot_both,
    act_both, act_send, act_recv, g_send, G, TT, GT, y_send, y_recv, x_send, x_recv, x_own,
    gw_tiles, cot_held, act_held, gt_held, local_sem, send_sem, recv_sem,
):
    row, col, dep = (lax.axis_index(name) for name in ("row", "col", "depth"))
    z, k = row // 2, lax.rem(row, 2)
    tau = 1 - 2 * k

    def device(dz=0, dx=0, dy=0, flip=False):
        core = 1 - k if flip else k
        return (2 * wrap(z + dz, RING) + core, wrap(col + dx, SIDE), wrap(dep + dy, SIDE))

    sibling = device(flip=True)
    numbers = {}
    groups = {}

    def number(key):
        return numbers.setdefault(key, len(numbers))

    def copy(group, key, source, target, to):
        return pltpu.make_async_remote_copy(
            src_ref=source, dst_ref=target,
            send_sem=send_sem.at[groups.setdefault(group, len(groups))],
            recv_sem=recv_sem.at[number(key)],
            device_id=to, device_id_type=pl.DeviceIdType.MESH,
        )

    def send(group, key, source, target, to):
        copy(group, key, source, target, to).start()

    def receive(key, size):
        copy("x", key, size, size, sibling).wait_recv()

    def all_sent(group, size):
        copy(group, ("x", 1), size, size, sibling).wait_send()

    def at_col(j):
        return wrap(col + j * tau, SIDE)

    def at_dep(j):
        return wrap(dep + j * tau, SIDE)

    def ring(j):
        return wrap(z + j * tau, RING)

    steps = (0, 2, 1, -1)

    def unit_group(i):
        return wrap(dep + steps[i], SIDE)

    def token_group(i):
        return wrap(dep - steps[i], SIDE)

    def lanes_of(i, half):
        return pl.ds(pl.multiple_of(unit_group(i) * CHUNK + half * HALF, HALF), HALF)

    local = [pltpu.make_async_copy(tok, T.at[dep, col], local_sem.at[0])]
    for i in range(SIDE):
        local.append(
            pltpu.make_async_copy(weight.at[:, lanes_of(i, k)], W.at[i], local_sem.at[1 + i])
        )
    local.append(pltpu.make_async_copy(weight.at[:, lanes_of(0, 1 - k)], W_rest, local_sem.at[5]))
    local.append(pltpu.make_async_copy(cot, cot_held, local_sem.at[6]))
    for transfer in local:
        transfer.start()

    partners = [device(dz=1), device(dz=-1), sibling]
    for step in range(1, SIDE):
        partners += [device(dx=step), device(dy=step)]
    barrier = pltpu.get_barrier_semaphore()
    for partner in partners:
        pl.semaphore_signal(barrier, inc=1, device_id=partner, device_id_type=pl.DeviceIdType.MESH)
    gap = jnp.zeros((PADDED - SHARE, HALF), f32)

    def padded(values):
        return jnp.concatenate([values, gap], axis=0).astype(bf16)

    pl.semaphore_wait(barrier, len(partners))

    for j in (1, -1, 2):
        send("x", ("x", j), tok, T.at[dep, col], device(dx=j * tau))
    send("k", "k", tok, T_sib.at[col], sibling)
    for i in range(SIDE):
        send("w", ("w", i), weight.at[:, lanes_of(i, 1 - k)], W_sib.at[i], sibling)
    for transfer in local:
        transfer.wait()
    for i in range(SIDE):
        cot_send[i] = padded(cot_held[:, lanes_of(i, 1 - k)].astype(f32))
        send("c", "c", cot_send.at[i], cot_recv.at[i], sibling)
    for j in (1, -1, 2):
        slot = T.at[dep, at_col(-j)]
        receive(("x", j), slot)
        send("k", "k" if j != 2 else "k2", slot, T_sib.at[at_col(-j)], sibling)
    for s in (1, -1):
        send("y", "y" if s == 1 else "ys", T.at[dep], T.at[dep], device(dy=s * tau))

    def relay_tokens():
        slot = T.at[at_dep(-1)]
        receive("y", slot)
        send("y", "ys", slot, slot, device(dy=tau))

    def partial_preact(i, columns):
        count = len(columns) * 2 * SUB

        def tile(n, carry):
            lanes = pl.ds(pl.multiple_of(n * TILE, TILE), TILE)
            own = jnp.stack([T[dep, at_col(j)] for j in columns]).reshape(count, HALF)
            other = jnp.stack([T_sib[at_col(j)] for j in columns]).reshape(count, HALF)
            total = jnp.dot(own, W[i, :, lanes], preferred_element_type=f32)
            total += jnp.dot(other, W_sib[i, :, lanes], preferred_element_type=f32)
            total = total.reshape(len(columns), 2, SUB, TILE)
            for n, j in enumerate(columns):
                part[i, at_col(j), :, :, lanes] = total[n]
            return carry

        lax.fori_loop(0, HALF // TILE, tile, 0)

    def of_block(i, block):
        return part[i, block // 2, lax.rem(block, 2)]

    def enter(i):
        first[i, 0] = of_block(i, ring(4)).astype(bf16)
        send("r", ("r", i, 1), first.at[i, 0], hop.at[i, 0], device(dz=tau))
        first[i, 1] = of_block(i, ring(-3)).astype(bf16)
        send("r", ("r", i, 1), first.at[i, 1], hop.at[i, 4], device(dz=-tau))

    def reduce_step(i, at):
        receive(("r", i, at), hop.at[i, pl.ds(0, 2 if at < 3 else 1)])
        for way in range(2 if at < 3 else 1):
            slot, j = (at - 1, 4 - at) if way == 0 else (3 + at, at - 3)
            later = 4 if slot + 1 in (3, 6) else at + 1
            hop[i, slot] = (hop[i, slot].astype(f32) + of_block(i, ring(j))).astype(bf16)
            send(
                "r", ("r", i, later), hop.at[i, slot], hop.at[i, slot + 1],
                device(dz=tau if way == 0 else -tau),
            )

    def spread(i, block, ways):
        slot = G.at[block, k, token_group(i)]
        for group, key, to in ways:
            send(group, key, slot, slot, to)

    def share(i, far):
        if far == 0:
            return ("s", 0)
        return ("s", far, (2, 0, 1, 1)[i])

    def begin(i):
        if i > 0:
            receive(("h", i), G.at[z, k, token_group(i)])
        spread(i, z, [
            ("g", ("g", i, 1), device(dz=tau)), ("g", ("g", i, 1), device(dz=-tau)),
            ("s", share(i, 0), sibling),
        ])

    def finish(i):
        receive(("r", i, 4), hop.at[i, pl.ds(0, 2)])
        v = of_block(i, z) + hop[i, 3].astype(f32) + hop[i, 6].astype(f32)
        cot_both[k] = cot_held[:, lanes_of(i, k)].astype(f32)
        cot_both[1 - k] = cot_recv[i].astype(f32)[:SHARE]
        given = cot_both[...].reshape(SUB, HALF)
        hyper = jnp.tanh(root_coef * (v + cubic_coef * v * v * v))
        inner = root_coef * (1.0 + 3.0 * cubic_coef * v * v)
        slope = 0.5 * (1.0 + hyper) + 0.5 * v * (1.0 - hyper * hyper) * inner
        gradient = (given * slope).astype(bf16)
        if i == 0:
            G[z, k, dep] = gradient
            begin(0)
        else:
            g_send[i] = gradient
            send("h", ("h", i), g_send.at[i], G.at[z, k, dep], device(dy=steps[i]))
        act_both[...] = (0.5 * v * (1.0 + hyper)).reshape(2, SHARE, HALF)
        act_held[:, lanes_of(i, k)] = act_both[k].astype(bf16)
        act_send[i] = padded(act_both[1 - k])
        send("a", "a", act_send.at[i], act_recv.at[i], sibling)

    def relay(i, far):
        receive(("g", i, far), hop.at[0, pl.ds(0, 2 if far < 4 else 1)])
        for way in range(2 if far < 4 else 1):
            ways = []
            if far < (4 if way == 0 else 3):
                ways.append(("g", ("g", i, far + 1), device(dz=tau if way == 0 else -tau)))
            ways.append(("s", share(i, far), sibling))
            spread(i, ring(-far if way == 0 else far), ways)

    def transpose(y):
        rows = T[y].reshape(RING * SUB, HALF)
        TT[:, y * RING * SUB : (y + 1) * RING * SUB] = rows.T

    def blocks(far):
        if far == 0:
            return [(0, z)]
        if far == 4:
            return [(7, ring(4))]
        return [(2 * far - 1, ring(-far)), (2 * far, ring(far))]

    def partial_tokens(far, streams):
        pieces = [(q, block, token_group(i)) for i in streams for q, block in blocks(far)]
        receive(share(streams[0], far), hop.at[0, pl.ds(0, len(pieces))])

        def tile(n, carry):
            at = pl.multiple_of(n * TILE, TILE)
            total = jnp.zeros((len(pieces) * SUB, TILE), f32)
            for half, right in ((k, W.at[0]), (1 - k, W_rest)):
                left = jnp.concatenate([G[block, half, group] for q, block, group in pieces], axis=0)
                total += lax.dot_general(
                    left, right[pl.ds(at, TILE)], (((1,), (1,)), ((), ())),
                    preferred_element_type=f32,
                )
            for m, (q, block, group) in enumerate(pieces):
                GT[q, group, :, pl.ds(at, TILE)] = total[m * SUB : (m + 1) * SUB]
            return carry

        lax.fori_loop(0, HALF // TILE, tile, 0)

    def send_piece(far, key, q, n, j, to):
        y_send[q, n] = GT[q, at_dep(j)].astype(bf16)
        send("p", key, y_send.at[q, n], y_recv.at[q, n], device(dy=to * tau))

    def stage_far_row(far):
        for q, block in blocks(far):
            send_piece(far, ("p", far, 0), q, 0, 2, 1)

    def stage_near_row(far):
        for q, block in blocks(far):
            send_piece(far, ("p", far, 1), q, 2, -1, -1)

    def block_one(far):
        partial_tokens(far, (1,))
        stage_far_row(far)

    def block_two(far):
        partial_tokens(far, (2, 3))
        stage_near_row(far)

    def block_pass(far):
        receive(("p", far, 0), hop.at[0, pl.ds(0, len(blocks(far)))])
        for q, block in blocks(far):
            y_recv[q, 0] = (y_recv[q, 0].astype(f32) + GT[q, at_dep(1)]).astype(bf16)
            send("p", ("p", far, 1), y_recv.at[q, 0], y_recv.at[q, 1], device(dy=tau))

    def block_end(far):
        receive(("p", far, 1), hop.at[0, pl.ds(0, 2 * len(blocks(far)))])
        for q, block in blocks(far):
            total = GT[q, dep]
            for n in (1, 2):
                total += y_recv[q, n].astype(f32)
            half, home = lax.rem(block, 2), block // 2
            away = wrap(home - col, SIDE)

            @pl.when(away == 0)
            def _():
                x_own[half] = total

            @pl.when(away != 0)
            def _():
                x_send[half, away - 1] = total.astype(bf16)
                send(
                    "home", "home", x_send.at[half, away - 1], x_recv.at[half, away - 1],
                    device(dx=away),
                )

    def write_tile(n):
        return pltpu.make_async_copy(
            gw_tiles.at[n], gw_out.at[:, pl.ds(pl.multiple_of(n * TILE, TILE), TILE)],
            local_sem.at[n],
        )

    def grad_weight(begin, end):
        def tile(n, carry):
            half = n // 3
            inner = pl.multiple_of(lax.rem(n, 3) * TILE, TILE)
            right = jnp.concatenate(
                [G[:, half, y, :, pl.ds(inner, TILE)].reshape(RING * SUB, TILE) for y in range(4)],
                axis=0,
            )
            gw_tiles[n] = jnp.dot(TT[...], right, preferred_element_type=f32).astype(bf16)
            write_tile(n).start()
            return carry

        lax.fori_loop(begin, end, tile, 0)

    write_act = pltpu.make_async_copy(act_held, act_out, local_sem.at[6])
    write_gt = pltpu.make_async_copy(gt_held, gt_out, local_sem.at[7])

    def activations():
        receive("a", act_recv)
        for i in range(SIDE):
            act_held[:, lanes_of(i, 1 - k)] = act_recv[i].astype(f32)[:SHARE].astype(bf16)
        write_act.start()

    turns = (1, 2, 3, 0)

    receive("k", T.at[0, pl.ds(0, 3)])
    receive(("w", turns[0]), W_sib.at[turns[0]])
    partial_preact(turns[0], (0, 1, -1))
    receive("k2", T.at[0, 0])
    partial_preact(turns[0], (2,))
    enter(turns[0])
    for i in turns[1:]:
        receive(("w", i), W_sib.at[i])
        partial_preact(i, (0, 1, -1, 2))
        enter(i)
    for i, at in ((1, 1), (2, 1), (3, 1), (1, 2), (0, 1)):
        reduce_step(i, at)
    relay_tokens()
    for i, at in ((2, 2), (3, 2), (1, 3), (0, 2), (2, 3), (3, 3)):
        reduce_step(i, at)
    receive("c", cot_recv)
    finish(1)
    reduce_step(0, 3)
    for i in (2, 3, 0):
        finish(i)
    for i in (1, 2, 3):
        begin(i)
    receive("ys", T.at[pl.ds(0, 2)])
    partial_tokens(0, (0, 1, 2, 3))
    stage_far_row(0)
    stage_near_row(0)
    for far in (1, 2, 3):
        relay(1, far)
        if far > 1:
            relay(0, far - 1)
        block_pass(far - 1)
        relay(2, far)
        block_one(far)
        relay(3, far)
        if far > 1:
            partial_tokens(far - 1, (0,))
        if far == 1:
            transpose(0)
            transpose(1)
        if far == 2:
            transpose(2)
            transpose(3)
        if far == 3:
            activations()
        block_two(far)
        block_end(far - 1)
    relay(1, 4)
    relay(0, 3)
    block_pass(3)
    relay(2, 4)
    block_one(4)
    relay(3, 4)
    partial_tokens(3, (0,))
    block_two(4)
    relay(0, 4)
    block_end(3)
    block_pass(4)
    partial_tokens(4, (0,))
    grad_weight(0, 2)
    block_end(4)
    grad_weight(2, 6)

    receive("home", hop.at[0, pl.ds(0, 6)])
    for half in range(2):
        total = x_own[half]
        for n in range(SIDE - 1):
            total += x_recv[half, n].astype(f32)
        gt_held[half] = total.astype(bf16)
    write_gt.start()
    for group, size in (
        ("x", T.at[0, pl.ds(0, 3)]), ("k", T.at[0]), ("w", W_sib), ("c", cot_recv),
        ("y", T.at[pl.ds(0, 3)]), ("r", hop), ("h", g_send.at[pl.ds(0, 3)]), ("g", hop),
        ("s", G.at[pl.ds(0, 4)]), ("a", act_recv), ("p", y_recv), ("home", x_send),
    ):
        all_sent(group, size)
    for n in range(CHUNK // TILE):
        write_tile(n).wait()
    write_act.wait()
    write_gt.wait()


def deliver(act, gt, gw, act_out, gt_out, gw_out, act_held, gt_held, gw_held, sem):
    moves = [(act, act_held, act_out), (gt, gt_held, gt_out)]
    for n in range(PIECES):
        rows = pl.ds(n * (HALF // PIECES), HALF // PIECES)
        moves.append((gw.at[rows], gw_held.at[rows], gw_out.at[rows]))
    into = [
        pltpu.make_async_copy(source, held, sem.at[0, n])
        for n, (source, held, target) in enumerate(moves)
    ]
    out_of = [
        pltpu.make_async_copy(held, target, sem.at[1, n])
        for n, (source, held, target) in enumerate(moves)
    ]
    for move in into:
        move.start()
    for arrived, move in zip(into, out_of):
        arrived.wait()
        move.start()
    for move in out_of:
        move.wait()


def on_device(tokens, weight, cotangent):
    scratch = [
        pltpu.VMEM((SIDE, SIDE, 2, SUB, HALF), bf16),
        pltpu.VMEM((SIDE, 2, SUB, HALF), bf16),
        pltpu.VMEM((SIDE, HALF, HALF), bf16),
        pltpu.VMEM((HALF, HALF), bf16),
        pltpu.VMEM((SIDE, HALF, HALF), bf16),
        pltpu.VMEM((SIDE, SIDE, 2, SUB, HALF), f32),
        pltpu.VMEM((SIDE, 7, SUB, HALF), bf16),
        pltpu.VMEM((SIDE, 2, SUB, HALF), bf16),
        pltpu.VMEM((SIDE, PADDED, HALF), bf16),
        pltpu.VMEM((SIDE, PADDED, HALF), bf16),
        pltpu.VMEM((2, SHARE, HALF), f32),
        pltpu.VMEM((2, SHARE, HALF), f32),
        pltpu.VMEM((SIDE, PADDED, HALF), bf16),
        pltpu.VMEM((SIDE, PADDED, HALF), bf16),
        pltpu.VMEM((SIDE, SUB, HALF), bf16),
        pltpu.VMEM((RING, 2, SIDE, SUB, HALF), bf16),
        pltpu.VMEM((HALF, RING * SIDE * SUB), bf16),
        pltpu.VMEM((RING, SIDE, SUB, HALF), f32),
        pltpu.VMEM((RING, 3, SUB, HALF), bf16),
        pltpu.VMEM((RING, 3, SUB, HALF), bf16),
        pltpu.VMEM((2, SIDE - 1, SUB, HALF), bf16),
        pltpu.VMEM((2, SIDE - 1, SUB, HALF), bf16),
        pltpu.VMEM((2, SUB, HALF), f32),
        pltpu.VMEM((CHUNK // TILE, HALF, TILE), bf16),
        pltpu.VMEM((SHARE, SIDE * CHUNK), bf16),
        pltpu.VMEM((SHARE, SIDE * CHUNK), bf16),
        pltpu.VMEM((2, SUB, HALF), bf16),
        pltpu.SemaphoreType.DMA((8,)),
        pltpu.SemaphoreType.DMA((12,)),
        pltpu.SemaphoreType.DMA((72,)),
    ]
    out_shape = (
        jax.ShapeDtypeStruct((SHARE, SIDE * CHUNK), bf16),
        jax.ShapeDtypeStruct((2, SUB, HALF), bf16),
        jax.ShapeDtypeStruct((HALF, CHUNK), bf16),
    )
    anywhere = pl.BlockSpec(memory_space=pl.ANY)
    results = pl.pallas_call(
        kernel,
        out_shape=out_shape,
        in_specs=[anywhere] * 3,
        out_specs=[anywhere] * 3,
        scratch_shapes=scratch,
        compiler_params=pltpu.CompilerParams(
            collective_id=0, has_side_effects=True, vmem_limit_bytes=60 * 2**20
        ),
        cost_estimate=pl.CostEstimate(
            flops=11 * 10**9, bytes_accessed=15 * 10**6, transcendentals=10**5
        ),
        name="gelu_grid",
    )(tokens.reshape(2, SUB, HALF), weight, cotangent)
    activated, grad_tokens, grad_weight = pl.pallas_call(
        deliver,
        out_shape=out_shape,
        in_specs=[anywhere] * 3,
        out_specs=[anywhere] * 3,
        scratch_shapes=[pltpu.VMEM(shape.shape, bf16) for shape in out_shape]
        + [pltpu.SemaphoreType.DMA((2, PIECES + 2))],
        name="deliver",
    )(*results)
    return activated, grad_tokens.reshape(2 * SUB, HALF), grad_weight


def solution(mesh):
    placed = (P(("depth", "col"), "row"), P("row", "col"), P(("depth", "row"), "col"))
    return jax.shard_map(
        on_device,
        mesh=mesh,
        in_specs=placed,
        out_specs=(
            P(("depth", "row"), "col"),
            P(("depth", "col"), "row"),
            P("row", ("col", "depth")),
        ),
        check_vma=False,
    )
```

```python
import functools
import math

import jax
import jax.numpy as jnp
from jax import lax
from jax.experimental import pallas as pl
from jax.experimental.pallas import tpu as pltpu
from jax.sharding import PartitionSpec as P

root_coef = math.sqrt(2.0 / math.pi)
cubic_coef = 0.044715

RING = 8
SIDE = 4
SUB = 48
HALF = 768
CHUNK = 2 * HALF
SHARE = 24
PADDED = 32
TILE = 256
f32, bf16 = jnp.float32, jnp.bfloat16


def wrap(value, extent):
    return lax.rem(value + 2 * extent, extent)


PIECES = 8


def kernel(
    tok, weight, cot, act_out, gt_out, gw_out,
    T, T_sib, W, W_rest, W_sib, part, hop, first, cot_send, cot_recv, cot_both,
    act_both, act_send, act_recv, g_send, G, TT, GT, y_send, y_recv, x_send, x_recv, x_own,
    gw_tiles, act_held, gt_held, local_sem, send_sem, recv_sem,
):
    row, col, dep = (lax.axis_index(name) for name in ("row", "col", "depth"))
    z, k = row // 2, lax.rem(row, 2)
    tau = 1 - 2 * k

    def device(dz=0, dx=0, dy=0, flip=False):
        core = 1 - k if flip else k
        return (2 * wrap(z + dz, RING) + core, wrap(col + dx, SIDE), wrap(dep + dy, SIDE))

    sibling = device(flip=True)
    numbers = {}
    groups = {}

    def number(key):
        return numbers.setdefault(key, len(numbers))

    def copy(group, key, source, target, to):
        return pltpu.make_async_remote_copy(
            src_ref=source, dst_ref=target,
            send_sem=send_sem.at[groups.setdefault(group, len(groups))],
            recv_sem=recv_sem.at[number(key)],
            device_id=to, device_id_type=pl.DeviceIdType.MESH,
        )

    def send(group, key, source, target, to):
        copy(group, key, source, target, to).start()

    def receive(key, size):
        copy("x", key, size, size, sibling).wait_recv()

    def all_sent(group, size):
        copy(group, ("x", 1), size, size, sibling).wait_send()

    def at_col(j):
        return wrap(col + j * tau, SIDE)

    def at_dep(j):
        return wrap(dep + j * tau, SIDE)

    def ring(j):
        return wrap(z + j * tau, RING)

    steps = (0, 2, 1, -1)

    def unit_group(i):
        return wrap(dep + steps[i], SIDE)

    def token_group(i):
        return wrap(dep - steps[i], SIDE)

    def lanes_of(i, half):
        return pl.ds(pl.multiple_of(unit_group(i) * CHUNK + half * HALF, HALF), HALF)

    local = [pltpu.make_async_copy(tok, T.at[dep, col], local_sem.at[0])]
    for i in range(SIDE):
        local.append(
            pltpu.make_async_copy(weight.at[:, lanes_of(i, k)], W.at[i], local_sem.at[1 + i])
        )
    local.append(pltpu.make_async_copy(weight.at[:, lanes_of(0, 1 - k)], W_rest, local_sem.at[5]))
    for transfer in local:
        transfer.start()

    partners = [device(dz=1), device(dz=-1), sibling]
    for step in range(1, SIDE):
        partners += [device(dx=step), device(dy=step)]
    barrier = pltpu.get_barrier_semaphore()
    for partner in partners:
        pl.semaphore_signal(barrier, inc=1, device_id=partner, device_id_type=pl.DeviceIdType.MESH)
    gap = jnp.zeros((PADDED - SHARE, HALF), f32)

    def padded(values):
        return jnp.concatenate([values, gap], axis=0).astype(bf16)

    pl.semaphore_wait(barrier, len(partners))

    for j in (1, -1, 2):
        send("x", ("x", j), tok, T.at[dep, col], device(dx=j * tau))
    send("k", "k", tok, T_sib.at[col], sibling)
    for i in range(SIDE):
        send("w", ("w", i), weight.at[:, lanes_of(i, 1 - k)], W_sib.at[i], sibling)
    for transfer in local:
        transfer.wait()
    for i in range(SIDE):
        cot_send[i] = padded(cot[:, lanes_of(i, 1 - k)].astype(f32))
        send("c", "c", cot_send.at[i], cot_recv.at[i], sibling)
    for j in (1, -1, 2):
        slot = T.at[dep, at_col(-j)]
        receive(("x", j), slot)
        send("k", "k" if j != 2 else "k2", slot, T_sib.at[at_col(-j)], sibling)
    for s in (1, -1):
        send("y", "y" if s == 1 else "ys", T.at[dep], T.at[dep], device(dy=s * tau))

    def relay_tokens():
        slot = T.at[at_dep(-1)]
        receive("y", slot)
        send("y", "ys", slot, slot, device(dy=tau))

    def partial_preact(i, columns):
        count = len(columns) * 2 * SUB

        def tile(n, carry):
            lanes = pl.ds(pl.multiple_of(n * TILE, TILE), TILE)
            own = jnp.stack([T[dep, at_col(j)] for j in columns]).reshape(count, HALF)
            other = jnp.stack([T_sib[at_col(j)] for j in columns]).reshape(count, HALF)
            total = jnp.dot(own, W[i, :, lanes], preferred_element_type=f32)
            total += jnp.dot(other, W_sib[i, :, lanes], preferred_element_type=f32)
            total = total.reshape(len(columns), 2, SUB, TILE)
            for n, j in enumerate(columns):
                part[i, at_col(j), :, :, lanes] = total[n]
            return carry

        lax.fori_loop(0, HALF // TILE, tile, 0)

    def of_block(i, block):
        return part[i, block // 2, lax.rem(block, 2)]

    def enter(i):
        first[i, 0] = of_block(i, ring(4)).astype(bf16)
        send("r", ("r", i, 1), first.at[i, 0], hop.at[i, 0], device(dz=tau))
        first[i, 1] = of_block(i, ring(-3)).astype(bf16)
        send("r", ("r", i, 1), first.at[i, 1], hop.at[i, 4], device(dz=-tau))

    def reduce_step(i, at):
        receive(("r", i, at), hop.at[i, pl.ds(0, 2 if at < 3 else 1)])
        for way in range(2 if at < 3 else 1):
            slot, j = (at - 1, 4 - at) if way == 0 else (3 + at, at - 3)
            later = 4 if slot + 1 in (3, 6) else at + 1
            hop[i, slot] = (hop[i, slot].astype(f32) + of_block(i, ring(j))).astype(bf16)
            send(
                "r", ("r", i, later), hop.at[i, slot], hop.at[i, slot + 1],
                device(dz=tau if way == 0 else -tau),
            )

    def spread(i, block, ways):
        slot = G.at[block, k, token_group(i)]
        for group, key, to in ways:
            send(group, key, slot, slot, to)

    def share(i, far):
        if far == 0:
            return ("s", 0)
        return ("s", far, (2, 0, 1, 1)[i])

    def begin(i):
        if i > 0:
            receive(("h", i), G.at[z, k, token_group(i)])
        spread(i, z, [
            ("g", ("g", i, 1), device(dz=tau)), ("g", ("g", i, 1), device(dz=-tau)),
            ("s", share(i, 0), sibling),
        ])

    def finish(i):
        receive(("r", i, 4), hop.at[i, pl.ds(0, 2)])
        v = of_block(i, z) + hop[i, 3].astype(f32) + hop[i, 6].astype(f32)
        cot_both[k] = cot[:, lanes_of(i, k)].astype(f32)
        cot_both[1 - k] = cot_recv[i].astype(f32)[:SHARE]
        given = cot_both[...].reshape(SUB, HALF)
        hyper = jnp.tanh(root_coef * (v + cubic_coef * v * v * v))
        inner = root_coef * (1.0 + 3.0 * cubic_coef * v * v)
        slope = 0.5 * (1.0 + hyper) + 0.5 * v * (1.0 - hyper * hyper) * inner
        gradient = (given * slope).astype(bf16)
        if i == 0:
            G[z, k, dep] = gradient
            begin(0)
        else:
            g_send[i] = gradient
            send("h", ("h", i), g_send.at[i], G.at[z, k, dep], device(dy=steps[i]))
        act_both[...] = (0.5 * v * (1.0 + hyper)).reshape(2, SHARE, HALF)
        act_held[:, lanes_of(i, k)] = act_both[k]
        act_send[i] = padded(act_both[1 - k])
        send("a", "a", act_send.at[i], act_recv.at[i], sibling)

    def relay(i, far):
        receive(("g", i, far), hop.at[0, pl.ds(0, 2 if far < 4 else 1)])
        for way in range(2 if far < 4 else 1):
            ways = []
            if far < (4 if way == 0 else 3):
                ways.append(("g", ("g", i, far + 1), device(dz=tau if way == 0 else -tau)))
            ways.append(("s", share(i, far), sibling))
            spread(i, ring(-far if way == 0 else far), ways)

    def transpose(y):
        rows = T[y].reshape(RING * SUB, HALF)
        TT[:, y * RING * SUB : (y + 1) * RING * SUB] = rows.T

    def blocks(far):
        if far == 0:
            return [(0, z)]
        if far == 4:
            return [(7, ring(4))]
        return [(2 * far - 1, ring(-far)), (2 * far, ring(far))]

    def partial_tokens(far, streams):
        pieces = [(q, block, token_group(i)) for i in streams for q, block in blocks(far)]
        receive(share(streams[0], far), hop.at[0, pl.ds(0, len(pieces))])

        def tile(n, carry):
            at = pl.multiple_of(n * TILE, TILE)
            total = jnp.zeros((len(pieces) * SUB, TILE), f32)
            for half, right in ((k, W.at[0]), (1 - k, W_rest)):
                left = jnp.concatenate([G[block, half, group] for q, block, group in pieces], axis=0)
                total += lax.dot_general(
                    left, right[pl.ds(at, TILE)], (((1,), (1,)), ((), ())),
                    preferred_element_type=f32,
                )
            for m, (q, block, group) in enumerate(pieces):
                GT[q, group, :, pl.ds(at, TILE)] = total[m * SUB : (m + 1) * SUB]
            return carry

        lax.fori_loop(0, HALF // TILE, tile, 0)

    def send_piece(far, key, q, n, j, to):
        y_send[q, n] = GT[q, at_dep(j)].astype(bf16)
        send("p", key, y_send.at[q, n], y_recv.at[q, n], device(dy=to * tau))

    def stage_far_row(far):
        for q, block in blocks(far):
            send_piece(far, ("p", far, 0), q, 0, 2, 1)

    def stage_near_row(far):
        for q, block in blocks(far):
            send_piece(far, ("p", far, 1), q, 2, -1, -1)

    def block_one(far):
        partial_tokens(far, (1,))
        stage_far_row(far)

    def block_two(far):
        partial_tokens(far, (2, 3))
        stage_near_row(far)

    def block_pass(far):
        receive(("p", far, 0), hop.at[0, pl.ds(0, len(blocks(far)))])
        for q, block in blocks(far):
            y_recv[q, 0] = (y_recv[q, 0].astype(f32) + GT[q, at_dep(1)]).astype(bf16)
            send("p", ("p", far, 1), y_recv.at[q, 0], y_recv.at[q, 1], device(dy=tau))

    def block_end(far):
        receive(("p", far, 1), hop.at[0, pl.ds(0, 2 * len(blocks(far)))])
        for q, block in blocks(far):
            total = GT[q, dep]
            for n in (1, 2):
                total += y_recv[q, n].astype(f32)
            half, home = lax.rem(block, 2), block // 2
            away = wrap(home - col, SIDE)

            @pl.when(away == 0)
            def _():
                x_own[half] = total

            @pl.when(away != 0)
            def _():
                x_send[half, away - 1] = total.astype(bf16)
                send(
                    "home", "home", x_send.at[half, away - 1], x_recv.at[half, away - 1],
                    device(dx=away),
                )

    def write_tile(n):
        return pltpu.make_async_copy(
            gw_tiles.at[n], gw_out.at[:, pl.ds(pl.multiple_of(n * TILE, TILE), TILE)],
            local_sem.at[n],
        )

    def grad_weight(begin, end):
        def tile(n, carry):
            half = n // 3
            inner = pl.multiple_of(lax.rem(n, 3) * TILE, TILE)
            right = jnp.concatenate(
                [G[:, half, y, :, pl.ds(inner, TILE)].reshape(RING * SUB, TILE) for y in range(4)],
                axis=0,
            )
            gw_tiles[n] = jnp.dot(TT[...], right, preferred_element_type=f32).astype(bf16)
            write_tile(n).start()
            return carry

        lax.fori_loop(begin, end, tile, 0)

    write_act = pltpu.make_async_copy(act_held, act_out, local_sem.at[6])
    write_gt = pltpu.make_async_copy(gt_held, gt_out, local_sem.at[7])

    def activations():
        receive("a", act_recv)
        for i in range(SIDE):
            act_held[:, lanes_of(i, 1 - k)] = act_recv[i].astype(f32)[:SHARE]
        write_act.start()

    turns = (1, 2, 3, 0)

    receive("k", T.at[0, pl.ds(0, 3)])
    receive(("w", turns[0]), W_sib.at[turns[0]])
    partial_preact(turns[0], (0, 1, -1))
    receive("k2", T.at[0, 0])
    partial_preact(turns[0], (2,))
    enter(turns[0])
    for i in turns[1:]:
        receive(("w", i), W_sib.at[i])
        partial_preact(i, (0, 1, -1, 2))
        enter(i)
    for i, at in ((1, 1), (2, 1), (3, 1), (1, 2), (0, 1)):
        reduce_step(i, at)
    relay_tokens()
    for i, at in ((2, 2), (3, 2), (1, 3), (0, 2), (2, 3), (3, 3)):
        reduce_step(i, at)
    receive("c", cot_recv)
    finish(1)
    reduce_step(0, 3)
    for i in (2, 3, 0):
        finish(i)
    for i in (1, 2, 3):
        begin(i)
    receive("ys", T.at[pl.ds(0, 2)])
    partial_tokens(0, (0, 1, 2, 3))
    stage_far_row(0)
    stage_near_row(0)
    for far in (1, 2, 3):
        relay(1, far)
        if far > 1:
            relay(0, far - 1)
        block_pass(far - 1)
        relay(2, far)
        block_one(far)
        relay(3, far)
        if far > 1:
            partial_tokens(far - 1, (0,))
        if far == 1:
            transpose(0)
            transpose(1)
        if far == 2:
            transpose(2)
            transpose(3)
        if far == 3:
            activations()
        block_two(far)
        block_end(far - 1)
    relay(1, 4)
    relay(0, 3)
    block_pass(3)
    relay(2, 4)
    block_one(4)
    relay(3, 4)
    partial_tokens(3, (0,))
    block_two(4)
    relay(0, 4)
    block_end(3)
    block_pass(4)
    partial_tokens(4, (0,))
    grad_weight(0, 2)
    block_end(4)
    grad_weight(2, 6)

    receive("home", hop.at[0, pl.ds(0, 6)])
    for half in range(2):
        total = x_own[half]
        for n in range(SIDE - 1):
            total += x_recv[half, n].astype(f32)
        gt_held[half] = total.astype(bf16)
    write_gt.start()
    for group, size in (
        ("x", T.at[0, pl.ds(0, 3)]), ("k", T.at[0]), ("w", W_sib), ("c", cot_recv),
        ("y", T.at[pl.ds(0, 3)]), ("r", hop), ("h", g_send.at[pl.ds(0, 3)]), ("g", hop),
        ("s", G.at[pl.ds(0, 4)]), ("a", act_recv), ("p", y_recv), ("home", x_send),
    ):
        all_sent(group, size)
    for n in range(CHUNK // TILE):
        write_tile(n).wait()
    write_act.wait()
    write_gt.wait()


def deliver(act, gt, gw, act_out, gt_out, gw_out, act_held, gt_held, gw_held, sem):
    arriving = pltpu.make_async_copy(act, act_held, sem.at[0, PIECES + 1])
    moves = [(gt, gt_held, gt_out)]
    for n in range(PIECES):
        rows = pl.ds(n * (HALF // PIECES), HALF // PIECES)
        moves.append((gw.at[rows], gw_held.at[rows], gw_out.at[rows]))
    into = [
        pltpu.make_async_copy(source, held, sem.at[0, n])
        for n, (source, held, target) in enumerate(moves)
    ]
    out_of = [
        pltpu.make_async_copy(held, target, sem.at[1, n])
        for n, (source, held, target) in enumerate(moves)
    ]
    for move in into:
        move.start()
    arriving.start()
    for n, (arrived, move) in enumerate(zip(into, out_of)):
        if n == PIECES // 2:
            arriving.wait()
            act_out[...] = act_held[...].astype(bf16)
        arrived.wait()
        move.start()
    for move in out_of:
        move.wait()


def on_device(tokens, weight, cotangent):
    scratch = [
        pltpu.VMEM((SIDE, SIDE, 2, SUB, HALF), bf16),
        pltpu.VMEM((SIDE, 2, SUB, HALF), bf16),
        pltpu.VMEM((SIDE, HALF, HALF), bf16),
        pltpu.VMEM((HALF, HALF), bf16),
        pltpu.VMEM((SIDE, HALF, HALF), bf16),
        pltpu.VMEM((SIDE, SIDE, 2, SUB, HALF), f32),
        pltpu.VMEM((SIDE, 7, SUB, HALF), bf16),
        pltpu.VMEM((SIDE, 2, SUB, HALF), bf16),
        pltpu.VMEM((SIDE, PADDED, HALF), bf16),
        pltpu.VMEM((SIDE, PADDED, HALF), bf16),
        pltpu.VMEM((2, SHARE, HALF), f32),
        pltpu.VMEM((2, SHARE, HALF), f32),
        pltpu.VMEM((SIDE, PADDED, HALF), bf16),
        pltpu.VMEM((SIDE, PADDED, HALF), bf16),
        pltpu.VMEM((SIDE, SUB, HALF), bf16),
        pltpu.VMEM((RING, 2, SIDE, SUB, HALF), bf16),
        pltpu.VMEM((HALF, RING * SIDE * SUB), bf16),
        pltpu.VMEM((RING, SIDE, SUB, HALF), f32),
        pltpu.VMEM((RING, 3, SUB, HALF), bf16),
        pltpu.VMEM((RING, 3, SUB, HALF), bf16),
        pltpu.VMEM((2, SIDE - 1, SUB, HALF), bf16),
        pltpu.VMEM((2, SIDE - 1, SUB, HALF), bf16),
        pltpu.VMEM((2, SUB, HALF), f32),
        pltpu.VMEM((CHUNK // TILE, HALF, TILE), bf16),
        pltpu.VMEM((SHARE, SIDE * CHUNK), f32),
        pltpu.VMEM((2, SUB, HALF), bf16),
        pltpu.SemaphoreType.DMA((8,)),
        pltpu.SemaphoreType.DMA((12,)),
        pltpu.SemaphoreType.DMA((72,)),
    ]
    out_shape = (
        jax.ShapeDtypeStruct((SHARE, SIDE * CHUNK), bf16),
        jax.ShapeDtypeStruct((2, SUB, HALF), bf16),
        jax.ShapeDtypeStruct((HALF, CHUNK), bf16),
    )
    held_act = jax.ShapeDtypeStruct((SHARE, SIDE * CHUNK), f32)
    anywhere = pl.BlockSpec(memory_space=pl.ANY)
    inside = pl.BlockSpec(memory_space=pltpu.VMEM)
    results = pl.pallas_call(
        kernel,
        out_shape=(held_act,) + out_shape[1:],
        in_specs=[anywhere, anywhere, inside],
        out_specs=[anywhere] * 3,
        scratch_shapes=scratch,
        compiler_params=pltpu.CompilerParams(
            collective_id=0, has_side_effects=True, vmem_limit_bytes=60 * 2**20
        ),
        cost_estimate=pl.CostEstimate(
            flops=11 * 10**9, bytes_accessed=15 * 10**6, transcendentals=10**5
        ),
        name="gelu_grid",
    )(tokens.reshape(2, SUB, HALF), weight, cotangent)
    activated, grad_tokens, grad_weight = pl.pallas_call(
        deliver,
        out_shape=out_shape,
        in_specs=[anywhere] * 3,
        out_specs=[inside, anywhere, anywhere],
        scratch_shapes=[
            pltpu.VMEM(shape.shape, shape.dtype) for shape in (held_act,) + out_shape[1:]
        ]
        + [pltpu.SemaphoreType.DMA((2, PIECES + 2))],
        name="deliver",
    )(*results)
    return activated, grad_tokens.reshape(2 * SUB, HALF), grad_weight


def solution(mesh):
    placed = (P(("depth", "col"), "row"), P("row", "col"), P(("depth", "row"), "col"))
    return jax.shard_map(
        on_device,
        mesh=mesh,
        in_specs=placed,
        out_specs=(
            P(("depth", "row"), "col"),
            P(("depth", "col"), "row"),
            P("row", ("col", "depth")),
        ),
        check_vma=False,
    )
```
